32 devices in a mesh: section: 4 (over y, core), peer: 8 (over z, x).
Axes of the slice: x: 2, y: 2, z: 4, core: 2. Of those that a mesh axis runs over, the one named last changes fastest.
Arguments:
- sent_rows: bfloat16 [4, 8, 128, 1024], P('section', 'peer'), may hold values from -6 to 6
- cotangent: bfloat16 [4, 8, 128, 1024], P('section', 'peer'), may hold values from -6 to 6
- wiring: int32 [4, 8], replicated, may hold values from 0 to 7, as said below
- w_qkv: bfloat16 [4, 1024, 3072], P('section')
- w_out: bfloat16 [4, 1024, 1024], P('section'), may hold values from -0.1875 to 0.1875
Outputs:
- layer_out: bfloat16 [4, 8, 2, 128, 1024], P('section', 'peer')
- input_grad: bfloat16 [4, 8, 128, 1024], P('section', 'peer')
- section_grad: float32 [4, 1024, 4096], P('section', 'peer')
The draws below stay inside these ranges and needn't reach their ends.
Inputs may be any that keep to these rules, and one draw needn't show every extreme that they name: In each row of wiring no peer is named more than 2 times, and some peer exactly 2 times.
All inputs are finite; a program needn't handle non-finite values.
Results may differ from the reference program's by a relative error of at most 0.0085.
Values may be sent and summed in bfloat16 or wider, within the bound.
No kernel may reach another device: no remote copies, remote signals or barrier semaphores. Data moves between devices by JAX's collectives and lax.ppermute only.
A program may use at most 128 MiB of HBM per device.

```python
import jax
import jax.numpy as jnp
from jax import lax

D = 1024
HEADS = 16
HEAD = 64
SEQ = 128
CAP = 2
SECTIONS = 4
PEERS = 8


def wire_single(key):
    first_key, second_key, third_key = jax.random.split(key, 3)
    busiest = jax.random.randint(first_key, (), 0, PEERS, dtype=jnp.int32)
    order = jax.random.permutation(second_key, 2 * PEERS - 2).astype(jnp.int32)
    labels = order // 2
    labels = labels + (labels >= busiest).astype(jnp.int32)
    chosen = jnp.concatenate([jnp.stack([busiest, busiest]), labels[:PEERS - 2]])
    return jax.random.permutation(third_key, chosen).astype(jnp.int32)


def draw_wiring(key, part):
    key = jax.random.fold_in(key, 5)
    section_keys = jax.random.split(key, SECTIONS)
    return jax.vmap(wire_single)(section_keys)


def draw_w_qkv(key, part):
    key = jax.random.fold_in(key, 11)
    base_key = jax.random.fold_in(key, 0)
    base = jax.random.normal(base_key, (SECTIONS, D, 3 * D), jnp.float32) * D ** (-0.5)
    return base.astype(jnp.bfloat16)


def with_spikes(result, stream_key, source, target, blocks, factor):
    owner, partner = [(jnp.arange(result.shape[axis_at]) // (result.shape[axis_at] // blocks)).reshape([-1 if axis == axis_at else 1 for axis in range(result.ndim)]) for axis_at in (source, target)]
    chosen = jax.random.permutation(stream_key, blocks)[partner]
    strong = (owner == chosen) | (owner == (partner + blocks // 2) % blocks)
    return jnp.where(strong, factor * result, result)


def level_of(own_key, shape, shards, smallest, high):
    level = 1.0
    for axis_at, parts in shards:
        draws = jax.random.uniform(jax.random.fold_in(jax.random.fold_in(own_key, 6), axis_at), (parts,), jnp.float32, smallest / len(shards), high / len(shards))
        level = level * jnp.repeat(jnp.exp(draws), shape[axis_at] // parts).reshape((-1,) + (1,) * (len(shape) - 1 - axis_at))
    return level


def gaussian(own_key, dims, spread, limit, cuts=(), held_as=jnp.bfloat16):
    level = level_of(own_key, dims, cuts, -0.22, 0.18) if cuts else 1.0
    array = jax.random.normal(own_key, dims, jnp.float32) * spread * level
    return jnp.minimum(jnp.maximum(array, -limit), limit).astype(held_as)


def noise_with(key, extent, scale, most, cuts, heavy, kind=jnp.bfloat16):
    drawn = scale * jax.random.normal(key, extent, jnp.float32)
    if cuts:
        drawn = drawn * level_of(key, extent, cuts, -0.22, 0.18)
    return jnp.clip(with_spikes(drawn, jax.random.fold_in(key, 3), *heavy), -most, most).astype(kind)


def setup_inputs(seed: int = 0) -> dict:
    seeds = jax.random.split(jax.random.key(seed), 6)
    return {
        "sent_rows": gaussian(seeds[0], (SECTIONS, PEERS, SEQ, D), 1.0, 6.0, ((0, 4), (1, 8))),
        "cotangent": noise_with(seeds[1], (SECTIONS, PEERS, SEQ, D), 1.0, 6.0, ((0, 4), (1, 8)), (1, 3, 8, 2.0)),
        "wiring": draw_wiring(jax.random.fold_in(seeds[5], 71), 0),
        "w_qkv": draw_w_qkv(jax.random.fold_in(seeds[5], 71), 0),
        "w_out": gaussian(seeds[4], (SECTIONS, D, D), D ** -0.5, 0.1875, ((0, 4),)),
    }


EPSILON = 1e-05

def slot_table(wire_row, peer_count, slot_count):
    match = (wire_row[:, None] == jnp.arange(peer_count, dtype=jnp.int32)[None, :]).astype(jnp.int32)
    before = jnp.cumsum(match, axis=0) - match
    ranked = lax.optimization_barrier(jnp.sum(before * match, axis=1))
    in_slot = (jnp.arange(slot_count, dtype=jnp.int32)[:, None] == ranked[None, :]).astype(jnp.int32)
    return jnp.transpose(match)[:, None, :] * in_slot[None, :, :]

def split_heads(rows):
    return rows.reshape(rows.shape[0], rows.shape[1], HEADS, HEAD)

def join_heads(rows):
    return rows.reshape(rows.shape[0], rows.shape[1], HEADS * HEAD)

def layer_pass(inputs, cotans, w_qkv, w_out):
    width = w_out.shape[0]
    score_scale = HEAD ** (-0.5)
    seq_len = inputs.shape[1]
    wide_in = inputs.astype(jnp.float32)
    inv_rms = lax.rsqrt(lax.optimization_barrier(jnp.mean(wide_in * wide_in, axis=-1, keepdims=True)) + EPSILON)
    normed = (wide_in * inv_rms).astype(jnp.bfloat16)
    project = jnp.einsum('btd,de->bte', normed.astype(jnp.float32), w_qkv.astype(jnp.float32)).astype(jnp.bfloat16)
    query_rows = split_heads(project[:, :, :width].astype(jnp.float32))
    key_rows = split_heads(project[:, :, width:2 * width].astype(jnp.float32))
    val_rows = split_heads(project[:, :, 2 * width:].astype(jnp.float32))
    position = jnp.arange(seq_len, dtype=jnp.int32)
    allowed = position[:, None] >= position[None, :]
    scores = jnp.einsum('bihe,bjhe->bhij', query_rows, key_rows) * score_scale
    scores = jnp.where(allowed[None, None], scores, -jnp.inf)
    top_score = lax.optimization_barrier(jnp.max(scores, axis=-1, keepdims=True))
    expo = jnp.exp(scores - top_score)
    attn_prob = expo / lax.optimization_barrier(jnp.sum(expo, axis=-1, keepdims=True))
    prob_bf = attn_prob.astype(jnp.bfloat16)
    attn_out = join_heads(jnp.einsum('bhij,bjhe->bihe', prob_bf.astype(jnp.float32), val_rows)).astype(jnp.bfloat16)
    mixed = jnp.einsum('bie,ed->bid', attn_out.astype(jnp.float32), w_out.astype(jnp.float32))
    layer_out = (wide_in + mixed).astype(jnp.bfloat16)
    cot_f = cotans.astype(jnp.float32)
    d_attn = jnp.einsum('bid,ed->bie', cot_f, w_out.astype(jnp.float32)).astype(jnp.bfloat16).astype(jnp.float32)
    d_attn_h = split_heads(d_attn)
    d_val = join_heads(jnp.einsum('bhij,bihe->bjhe', prob_bf.astype(jnp.float32), d_attn_h)).astype(jnp.bfloat16)
    d_prob = jnp.einsum('bihe,bjhe->bhij', d_attn_h, val_rows)
    d_score = (attn_prob * (d_prob - lax.optimization_barrier(jnp.sum(d_prob * attn_prob, axis=-1, keepdims=True))) * score_scale).astype(jnp.bfloat16).astype(jnp.float32)
    d_query = join_heads(jnp.einsum('bhij,bjhe->bihe', d_score, key_rows)).astype(jnp.bfloat16)
    d_key = join_heads(jnp.einsum('bhij,bihe->bjhe', d_score, query_rows)).astype(jnp.bfloat16)
    grad_proj = jnp.concatenate([d_query, d_key, d_val], axis=-1)
    d_normed = jnp.einsum('bte,de->btd', grad_proj.astype(jnp.float32), w_qkv.astype(jnp.float32))
    input_grad = (cot_f + inv_rms * d_normed - wide_in * inv_rms ** 3 * lax.optimization_barrier(jnp.mean(d_normed * wide_in, axis=-1, keepdims=True))).astype(jnp.bfloat16)
    return (layer_out, input_grad, normed, grad_proj, attn_out)

def grad_terms(normed, cotans, grad_proj, attn_out):
    first = jnp.einsum('bti,bte->ie', normed.astype(jnp.float32), grad_proj.astype(jnp.float32))
    second = jnp.einsum('bti,bth->ih', cotans.astype(jnp.float32), attn_out.astype(jnp.float32))
    return jnp.concatenate([first, second], axis=1)

def reference(sent_rows, cotangent, wiring, w_qkv, w_out):

    def per_section(section):
        source = (section + SECTIONS - 1) % SECTIONS
        inputs = sent_rows[source]
        cotans = cotangent[source]
        layer_out, input_grad, normed, grad_proj, attn_out = layer_pass(inputs, cotans, w_qkv[section], w_out[section])
        summed = grad_terms(normed, cotans, grad_proj, attn_out) / PEERS
        select = slot_table(wiring[source], PEERS, CAP).astype(jnp.float32)
        slotted = jnp.einsum('rcq,qtd->rctd', select, layer_out.astype(jnp.float32)).astype(jnp.bfloat16)
        return (slotted, input_grad, summed)
    slotted, input_grad, summed = lax.map(per_section, jnp.arange(SECTIONS, dtype=jnp.int32))
    return (slotted, jnp.roll(input_grad, -1, axis=0), summed)
```

```python
import jax
import jax.numpy as jnp
from jax import lax
from jax.sharding import PartitionSpec as P

HEADS = 16
HEAD = 64
CAP = 2
EPSILON = 1e-05
BF = jnp.bfloat16
F32 = jnp.float32


def slot_sources(wire_row, peer_count, slot_count):
    match = (wire_row[:, None] == jnp.arange(peer_count, dtype=jnp.int32)[None, :]).astype(jnp.int32)
    before = jnp.cumsum(match, axis=0) - match
    ranked = jnp.sum(before * match, axis=1)
    in_slot = (jnp.arange(slot_count, dtype=jnp.int32)[:, None] == ranked[None, :]).astype(jnp.int32)
    table = jnp.transpose(match)[:, None, :] * in_slot[None, :, :]
    number = jnp.arange(1, peer_count + 1, dtype=jnp.int32)
    return jnp.sum(table * number, axis=-1) - 1


def split_heads(rows):
    return rows.reshape(rows.shape[0], HEADS, HEAD)


def join_heads(rows):
    return rows.reshape(rows.shape[0], HEADS * HEAD)


def normalize(rows):
    wide = rows.astype(F32)
    inv_rms = lax.rsqrt(jnp.mean(wide * wide, axis=-1, keepdims=True) + EPSILON)
    return wide, inv_rms, (wide * inv_rms).astype(BF)


def dot(a, b, dims):
    return lax.dot_general(a, b, (dims, ((), ())), preferred_element_type=F32)


def shards(sent_rows, cotangent, wiring, w_qkv, w_out):
    peers = lax.axis_size("peer")
    sections = lax.axis_size("section")
    depth = peers // 2
    me = lax.axis_index("peer")
    row, col = me // 2, me % 2
    weights_in, weights_back = w_qkv[0], w_out[0]
    width = weights_back.shape[0]
    block = width // depth
    third = width // depth

    def hop(value, steps):
        pairs = [
            (s * peers + p, (s + 1) % sections * peers + (p + 2 * steps) % peers)
            for s in range(sections)
            for p in range(peers)
        ]
        return lax.ppermute(value, ("section", "peer"), pairs)

    def along(value, steps):
        return lax.ppermute(value, "peer", [(p, (p + 2 * steps) % peers) for p in range(peers)])

    def across(value):
        return lax.ppermute(value, "peer", [(p, p ^ 1) for p in range(peers)])

    sent, cot = sent_rows[0, 0], cotangent[0, 0]
    x = hop(sent, 0)
    g = hop(cot, 0)
    column_x = [x] + [hop(sent, k) for k in range(1, depth)]
    cot_blocks = cot.reshape(cot.shape[0], depth, block)

    def cot_block(k):
        return lax.dynamic_index_in_dim(cot_blocks, (row + k) % depth, 1, keepdims=False)

    column_g = [hop(cot_block(k), k) for k in range(depth)]

    wide, inv_rms, normed = normalize(x)
    seq_len = x.shape[0]
    project = dot(normed, weights_in, ((1,), (0,))).astype(BF)
    query, key, val = (split_heads(project[:, i * width : (i + 1) * width]) for i in range(3))
    position = jnp.arange(seq_len, dtype=jnp.int32)
    allowed = position[:, None] >= position[None, :]
    scale = HEAD ** (-0.5)
    scores = jnp.einsum("ihe,jhe->hij", query, key, preferred_element_type=F32) * scale
    scores = jnp.where(allowed[None], scores, -jnp.inf)
    expo = jnp.exp(scores - jnp.max(scores, axis=-1, keepdims=True))
    prob = expo / jnp.sum(expo, axis=-1, keepdims=True)
    prob_bf = prob.astype(BF)
    attn = join_heads(jnp.einsum("hij,jhe->ihe", prob_bf, val, preferred_element_type=F32)).astype(BF)
    d_attn = split_heads(dot(g, weights_back, ((1,), (1,))).astype(BF))
    d_val = join_heads(jnp.einsum("hij,ihe->jhe", prob_bf, d_attn, preferred_element_type=F32)).astype(BF)
    d_prob = jnp.einsum("ihe,jhe->hij", d_attn, val, preferred_element_type=F32)
    d_score = (prob * (d_prob - jnp.sum(d_prob * prob, axis=-1, keepdims=True)) * scale).astype(BF)
    d_query = join_heads(jnp.einsum("hij,jhe->ihe", d_score, key, preferred_element_type=F32)).astype(BF)
    d_key = join_heads(jnp.einsum("hij,ihe->jhe", d_score, query, preferred_element_type=F32)).astype(BF)
    grads = [d_query, d_key, d_val]

    by_block = jnp.stack([t.reshape(seq_len, depth, third) for t in grads])

    def grad_block(k):
        return lax.dynamic_index_in_dim(by_block, (row + k) % depth, 2, keepdims=False)

    column_d = [grad_block(0)] + [along(grad_block(k), k) for k in range(1, depth)]
    column_attn = [attn] + [along(attn, k) for k in range(1, depth)]

    d_normed = dot(jnp.concatenate(grads, axis=1), weights_in, ((1,), (1,)))
    input_grad = (
        g.astype(F32)
        + inv_rms * d_normed
        - wide * inv_rms**3 * jnp.mean(d_normed * wide, axis=-1, keepdims=True)
    ).astype(BF)
    back = lax.ppermute(input_grad, "section", [(s, (s - 1) % sections) for s in range(sections)])

    normed_all = jnp.concatenate([normalize(t)[2] for t in column_x], axis=0)
    d_all = jnp.concatenate(column_d, axis=1)
    partial = jnp.einsum("ti,cte->ice", normed_all, d_all, preferred_element_type=F32) / peers
    slab = width // peers
    partial = partial.reshape(depth, 2, slab, 3, third)
    mine = lax.dynamic_index_in_dim(partial, col, 1, keepdims=False)
    other = lax.dynamic_index_in_dim(partial, 1 - col, 1, keepdims=False).astype(BF)
    summed = (mine + across(other).astype(F32)).astype(BF)
    groups = [[2 * a + c for a in range(depth)] for c in range(2)]
    landed = lax.all_to_all(summed, "peer", 0, 0, axis_index_groups=groups, tiled=True)
    first = jnp.transpose(landed, (1, 2, 0, 3)).reshape(slab, 3 * width).astype(F32)

    attn_all = jnp.concatenate(column_attn, axis=0)
    g_all = jnp.concatenate(column_g, axis=0)
    out_part = dot(g_all, attn_all, ((0,), (0,))) / peers
    out_part = out_part.reshape(2, slab, width)
    out_mine = lax.dynamic_index_in_dim(out_part, col, 0, keepdims=False)
    out_other = lax.dynamic_index_in_dim(out_part, 1 - col, 0, keepdims=False).astype(BF)
    second = out_mine + across(out_other).astype(F32)
    section_grad = jnp.concatenate([first, second], axis=1)

    source = (lax.axis_index("section") + sections - 1) % sections
    wire_row = lax.dynamic_index_in_dim(wiring, source, 0, keepdims=False)
    table = slot_sources(wire_row, peers, CAP)
    x_stack = jnp.stack(column_x)
    attn_stack = jnp.stack(column_attn)

    def slots_of(peer):
        taken = lax.dynamic_index_in_dim(table, peer, 0, keepdims=False)
        here = (taken >= 0) & (taken % 2 == col)
        place = jnp.where(here, (row - taken // 2) % depth, 0)
        pick = [
            [lax.dynamic_index_in_dim(s, place[c], 0, keepdims=False) for c in range(CAP)]
            for s in (x_stack, attn_stack)
        ]
        return here, pick

    here_mine, picks_mine = slots_of(me)
    here_other, picks_other = slots_of(me ^ 1)
    here = jnp.concatenate([here_mine, here_other])
    x_pick = jnp.concatenate(picks_mine[0] + picks_other[0], axis=0)
    attn_pick = jnp.concatenate(picks_mine[1] + picks_other[1], axis=0)
    y = (x_pick.astype(F32) + dot(attn_pick, weights_back, ((1,), (0,)))).astype(BF)
    y = y.reshape(2 * CAP, seq_len, width)
    y = jnp.where(here[:, None, None], y, jnp.zeros((), BF))
    layer_out = y[:CAP] + across(y[CAP:])
    return (layer_out[None, None], back[None, None], section_grad[None])


def solution(mesh):
    in_specs = (
        P("section", "peer", None, None),
        P("section", "peer", None, None),
        P(),
        P("section", None, None),
        P("section", None, None),
    )
    out_specs = (
        P("section", "peer", None, None, None),
        P("section", "peer", None, None),
        P("section", "peer", None),
    )
    return jax.shard_map(shards, mesh=mesh, in_specs=in_specs, out_specs=out_specs, check_vma=False)
```

```python
import functools

import jax
import jax.numpy as jnp
from jax import lax
from jax.experimental import pallas as pl
from jax.experimental.pallas import tpu as pltpu
from jax.sharding import PartitionSpec as P

HEAD = 64
CAP = 2
EPSILON = 1e-05
LANES = 128
BF = jnp.bfloat16
F32 = jnp.float32
MIB = 1 << 20


def dot(a, b, dims=((1,), (0,))):
    return lax.dot_general(a, b, (dims, ((), ())), preferred_element_type=F32)


def inverse_rms(wide):
    return lax.rsqrt(jnp.mean(wide * wide, axis=-1, keepdims=True) + EPSILON)


def whole(shape):
    return pl.BlockSpec(shape, lambda *_: (0,) * len(shape))


def call(body, name, ids, arrays, in_specs, out_shapes, out_specs, grid=(1,), scratch=(), flops=0, nbytes=0):
    spec = pltpu.PrefetchScalarGridSpec(
        num_scalar_prefetch=len(ids),
        grid=grid,
        in_specs=in_specs,
        out_specs=out_specs,
        scratch_shapes=list(scratch),
    )
    return pl.pallas_call(
        body,
        grid_spec=spec,
        out_shape=out_shapes,
        name=name,
        compiler_params=pltpu.CompilerParams(vmem_limit_bytes=40 * MIB),
        cost_estimate=pl.CostEstimate(flops=flops, bytes_accessed=nbytes, transcendentals=0),
    )(*ids, *arrays)


def shape(dims, dtype=BF):
    return jax.ShapeDtypeStruct(dims, dtype)


def layer_body(depth, ids, x_ref, g_ref, wq_ref, wk_ref, wv_ref, wo_ref, *rest):
    attn_ref, grad_refs, normed_ref = rest[0], rest[1 : 1 + depth], rest[1 + depth]
    step = pl.program_id(0)
    seq = x_ref.shape[0]
    scale = HEAD ** (-0.5)

    @pl.when(step == 0)
    def _():
        wide = x_ref[...].astype(F32)
        normed_ref[...] = (wide * inverse_rms(wide)).astype(BF)

    normed = normed_ref[...]
    query = dot(normed, wq_ref[...]).astype(BF)
    key = dot(normed, wk_ref[...]).astype(BF)
    val = dot(normed, wv_ref[...]).astype(BF)
    d_attn = dot(g_ref[...], wo_ref[...], ((1,), (1,))).astype(BF)
    low = lax.broadcasted_iota(jnp.int32, (seq, LANES), 1) < HEAD
    rows = lax.broadcasted_iota(jnp.int32, (2 * seq, seq), 0)
    allowed = jnp.where(rows < seq, rows, rows - seq) >= lax.broadcasted_iota(jnp.int32, (2 * seq, seq), 1)
    zero = jnp.zeros((), BF)

    def both(value):
        return jnp.concatenate([jnp.where(low, value, zero), jnp.where(low, zero, value)], axis=0)

    def merge(value):
        return jnp.where(low, value[:seq], value[seq:]).astype(BF)

    results = []
    for pair in range(query.shape[1] // LANES):
        cut = slice(pair * LANES, (pair + 1) * LANES)
        k, v = key[:, cut], val[:, cut]
        q2, da2 = both(query[:, cut]), both(d_attn[:, cut])
        scores = jnp.where(allowed, dot(q2, k, ((1,), (1,))) * scale, -jnp.inf)
        expo = jnp.exp(scores - jnp.max(scores, axis=-1, keepdims=True))
        prob = expo / jnp.sum(expo, axis=-1, keepdims=True)
        prob_bf = prob.astype(BF)
        attn_ref[:, cut] = merge(dot(prob_bf, v))
        d_val = dot(prob_bf, da2, ((0,), (0,))).astype(BF)
        d_prob = dot(da2, v, ((1,), (1,)))
        d_score = prob * (d_prob - jnp.sum(d_prob * prob, axis=-1, keepdims=True)) * scale
        d_score = d_score.astype(BF)
        d_query = merge(dot(d_score, k))
        d_key = dot(d_score, q2, ((0,), (0,))).astype(BF)
        results.append((cut, d_query, d_key, d_val))

    for k, grad_ref in enumerate(grad_refs):

        @pl.when(step == k)
        def _():
            for cut, *parts in results:
                for c, part in enumerate(parts):
                    grad_ref[c, :, cut] = part


def input_grad_body(depth, ids, x_ref, g_ref, wq_ref, wk_ref, wv_ref, *rest):
    grad_refs, out_ref, total_ref = rest[:depth], rest[depth], rest[depth + 1]
    step = pl.program_id(0)

    @pl.when(step == 0)
    def _():
        total_ref[...] = jnp.zeros_like(total_ref)

    for k, grad_ref in enumerate(grad_refs):

        @pl.when(step == k)
        def _():
            total_ref[...] += (
                dot(grad_ref[0], wq_ref[...], ((1,), (1,)))
                + dot(grad_ref[1], wk_ref[...], ((1,), (1,)))
                + dot(grad_ref[2], wv_ref[...], ((1,), (1,)))
            )

    @pl.when(step == depth - 1)
    def _():
        wide = x_ref[...].astype(F32)
        inv_rms = inverse_rms(wide)
        d_normed = total_ref[...]
        mean = jnp.mean(d_normed * wide, axis=-1, keepdims=True)
        grad = g_ref[...].astype(F32) + inv_rms * d_normed - wide * inv_rms**3 * mean
        out_ref[...] = grad.astype(BF)


def normed_body(depth, *refs):
    x_refs, out_ref = refs[:depth], refs[depth]
    seq = x_refs[0].shape[0]
    for k, x_ref in enumerate(x_refs):
        wide = x_ref[...].astype(F32)
        out_ref[:, k * seq : (k + 1) * seq] = jnp.transpose(wide * inverse_rms(wide)).astype(BF)


def proj_grad_body(depth, peers, added, ids, normed_ref, *refs):
    grad_refs, rest = refs[:depth], refs[depth:]
    out_ref, stack_ref = rest[-2], rest[-1]
    thirds, seq, block = grad_refs[0].shape
    for k, grad_ref in enumerate(grad_refs):
        for c in range(thirds):
            stack_ref[k * seq : (k + 1) * seq, c * block : (c + 1) * block] = grad_ref[c]
    left = normed_ref[...].reshape(-1, depth * seq)
    part = dot(left, stack_ref[...]).reshape(out_ref.shape) * (1.0 / peers)
    if added:
        part = part + rest[0][...].astype(F32)
    out_ref[...] = part.astype(BF)


def out_grad_body(depth, peers, ids, *refs):
    g_refs, attn_refs = refs[:depth], refs[depth : 2 * depth]
    mine_ref, other_ref, total_ref = refs[2 * depth :]
    slab = mine_ref.shape[0]
    total = dot(g_refs[0][...], attn_refs[0][...], ((0,), (0,)))
    for g_ref, attn_ref in zip(g_refs[1:], attn_refs[1:]):
        total += dot(g_ref[...], attn_ref[...], ((0,), (0,)))
    total_ref[...] = total * (1.0 / peers)
    col = ids[2]
    mine_ref[...] = total_ref[pl.ds(pl.multiple_of(col * slab, slab), slab), :]
    other_ref[...] = total_ref[pl.ds(pl.multiple_of((1 - col) * slab, slab), slab), :].astype(BF)


def slots_body(depth, peers, sections, across, ids, wiring, *refs):
    x_refs, attn_refs, w_ref = refs[:depth], refs[depth : 2 * depth], refs[2 * depth]
    rest = refs[2 * depth + 1 :]
    out_ref, x_pick, attn_pick = rest[-3:]
    section, row, col = ids[0], ids[1], ids[2]
    target = 2 * row + (1 - col if across else col)
    source = lax.rem(section + sections - 1, sections)
    seq = x_refs[0].shape[0]
    count = jnp.int32(0)
    taken = [jnp.int32(-1)] * CAP
    for p in range(peers):
        hit = wiring[source, p] == target
        for c in range(CAP):
            taken[c] = jnp.where(hit & (count == c), p, taken[c])
        count = count + hit.astype(jnp.int32)
    here = [(t >= 0) & (lax.rem(t, 2) == col) for t in taken]
    for c in range(CAP):
        part = slice(c * seq, (c + 1) * seq)
        place = lax.rem(row - lax.div(taken[c], 2) + depth, depth)
        for k in range(depth):

            @pl.when(here[c] & (place == k))
            def _():
                x_pick[part, :] = x_refs[k][...]
                attn_pick[part, :] = attn_refs[k][...]

        @pl.when(jnp.logical_not(here[c]))
        def _():
            x_pick[part, :] = jnp.zeros((seq, x_pick.shape[1]), BF)
            attn_pick[part, :] = jnp.zeros((seq, attn_pick.shape[1]), BF)

    y = (x_pick[...].astype(F32) + dot(attn_pick[...], w_ref[...])).astype(BF)
    for c in range(CAP):
        part = y[c * seq : (c + 1) * seq]
        out_ref[c] = part if across else part + rest[0][c]


def final_body(depth, landed_ref, mine_ref, received_ref, out_ref):
    step = pl.program_id(0)
    block = landed_ref.shape[2]

    @pl.when(step < 3)
    def _():
        for a in range(depth):
            out_ref[:, a * block : (a + 1) * block] = landed_ref[a].astype(F32)

    @pl.when(step == 3)
    def _():
        out_ref[...] = mine_ref[...] + received_ref[...].astype(F32)


def shards(sent_rows, cotangent, wiring, w_qkv, w_out):
    peers = lax.axis_size("peer")
    sections = lax.axis_size("section")
    depth = peers // 2
    me = lax.axis_index("peer")
    row, col = me // 2, me % 2
    ids = jnp.stack([lax.axis_index("section"), row, col]).astype(jnp.int32)
    weights_in, weights_back = w_qkv[0], w_out[0]
    width = weights_back.shape[0]
    block = width // depth
    slab = width // peers
    seq = sent_rows.shape[2]

    def hop(value, steps):
        pairs = [
            (s * peers + p, (s + 1) % sections * peers + (p + 2 * steps) % peers)
            for s in range(sections)
            for p in range(peers)
        ]
        return lax.ppermute(value, ("section", "peer"), pairs)

    def along(value, steps):
        return lax.ppermute(value, "peer", [(p, (p + 2 * steps) % peers) for p in range(peers)])

    def across(value):
        return lax.ppermute(value, "peer", [(p, p ^ 1) for p in range(peers)])

    x = hop(sent_rows[0, 0], 0)
    g = hop(cotangent[0, 0], 0)
    column_x = [x] + [along(x, k) for k in range(1, depth)]

    def group(third):
        return lambda k, ids: (0, third * depth + lax.rem(ids[1] + k, depth))

    seq_spec = whole((seq, width))
    w_specs = [pl.BlockSpec((width, block), group(third)) for third in range(3)]
    w_bytes = 2 * width * 3 * width
    attn, *grads = call(
        functools.partial(layer_body, depth),
        "layer",
        (ids,),
        (x, g, weights_in, weights_in, weights_in, weights_back),
        [seq_spec, seq_spec, *w_specs, pl.BlockSpec((block, width), lambda k, ids: (lax.rem(ids[1] + k, depth), 0))],
        [shape((seq, width))] + [shape((3, seq, block))] * depth,
        [pl.BlockSpec((seq, block), lambda k, ids: (0, lax.rem(ids[1] + k, depth)))] + [whole((3, seq, block))] * depth,
        grid=(depth,),
        scratch=[pltpu.VMEM((seq, width), BF)],
        flops=12 * seq * width * width,
        nbytes=w_bytes + 2 * width * width,
    )
    column_d = [grads[0]] + [along(grads[k], k) for k in range(1, depth)]
    column_attn = [attn] + [along(attn, k) for k in range(1, depth)]

    input_grad = call(
        functools.partial(input_grad_body, depth),
        "input_grad",
        (ids,),
        (x, g, weights_in, weights_in, weights_in, *grads),
        [seq_spec, seq_spec, *w_specs] + [whole((3, seq, block))] * depth,
        shape((seq, width)),
        seq_spec,
        grid=(depth,),
        scratch=[pltpu.VMEM((seq, width), F32)],
        flops=6 * seq * width * width,
        nbytes=w_bytes,
    )
    back = lax.ppermute(input_grad, "section", [(s, (s - 1) % sections) for s in range(sections)])

    normed = call(
        functools.partial(normed_body, depth),
        "normed",
        (),
        column_x,
        [seq_spec] * depth,
        shape((width, depth * seq)),
        whole((width, depth * seq)),
        flops=6 * depth * seq * width,
        nbytes=4 * depth * seq * width,
    )
    normed = normed.reshape(depth, 2, slab, depth * seq)

    def proj_grad(mine, extra):
        return call(
            functools.partial(proj_grad_body, depth, peers, mine),
            "proj_grad",
            (ids,),
            (normed, *column_d, *extra),
            [
                pl.BlockSpec(
                    (depth, None, slab, depth * seq),
                    (lambda k, ids: (0, ids[2], 0, 0)) if mine else (lambda k, ids: (0, 1 - ids[2], 0, 0)),
                )
            ]
            + [whole((3, seq, block))] * depth
            + [whole((depth, slab, 3 * block))] * len(extra),
            shape((depth, slab, 3 * block)),
            whole((depth, slab, 3 * block)),
            scratch=[pltpu.VMEM((depth * seq, 3 * block), BF)],
            flops=2 * depth * slab * depth * seq * 3 * block,
            nbytes=2 * (depth * slab * depth * seq + depth * seq * 3 * block + depth * slab * 3 * block),
        )

    received = across(proj_grad(False, ()))
    summed = proj_grad(True, (received,))
    groups = [[2 * a + c for a in range(depth)] for c in range(2)]
    landed = lax.all_to_all(summed, "peer", 0, 0, axis_index_groups=groups, tiled=True)

    cot_blocks = cotangent[0, 0].reshape(seq, depth, block)
    column_g = [
        hop(lax.dynamic_index_in_dim(cot_blocks, (row + k) % depth, 1, keepdims=False), k) for k in range(depth)
    ]
    out_mine, out_other = call(
        functools.partial(out_grad_body, depth, peers),
        "out_grad",
        (ids,),
        (*column_g, *column_attn),
        [whole((seq, block))] * depth + [seq_spec] * depth,
        [shape((slab, width), F32), shape((slab, width))],
        [whole((slab, width))] * 2,
        scratch=[pltpu.VMEM((block, width), F32)],
        flops=2 * depth * seq * block * width,
        nbytes=2 * depth * seq * (block + width),
    )
    out_received = across(out_other)

    def slots(to_neighbour, extra):
        return call(
            functools.partial(slots_body, depth, peers, sections, to_neighbour),
            "slots",
            (ids, wiring),
            (*column_x, *column_attn, weights_back, *extra),
            [seq_spec] * (2 * depth) + [whole((width, width))] + [whole((CAP, seq, width))] * len(extra),
            shape((CAP, seq, width)),
            whole((CAP, seq, width)),
            scratch=[pltpu.VMEM((CAP * seq, width), BF)] * 2,
            flops=2 * CAP * seq * width * width,
            nbytes=2 * (width * width + 4 * depth * seq * width),
        )

    layer_out = slots(False, (across(slots(True, ())),))

    section_grad = call(
        functools.partial(final_body, depth),
        "final",
        (),
        (landed, out_mine, out_received),
        [pl.BlockSpec((depth, slab, block), lambda c: (0, 0, jnp.minimum(c, 2)))] + [whole((slab, width))] * 2,
        shape((slab, 4 * width), F32),
        pl.BlockSpec((slab, width), lambda c: (0, c)),
        grid=(4,),
        nbytes=8 * slab * 4 * width,
    )
    return (layer_out[None, None], back[None, None], section_grad[None])


def solution(mesh):
    in_specs = (
        P("section", "peer", None, None),
        P("section", "peer", None, None),
        P(),
        P("section", None, None),
        P("section", None, None),
    )
    out_specs = (
        P("section", "peer", None, None, None),
        P("section", "peer", None, None),
        P("section", "peer", None),
    )
    return jax.shard_map(shards, mesh=mesh, in_specs=in_specs, out_specs=out_specs, check_vma=False)
```

```python
import functools

import jax
import jax.numpy as jnp
from jax import lax
from jax.experimental import pallas as pl
from jax.experimental.pallas import tpu as pltpu
from jax.sharding import PartitionSpec as P

HEAD = 64
CAP = 2
EPSILON = 1e-05
LANES = 128
BF = jnp.bfloat16
F32 = jnp.float32
MIB = 1 << 20


def dot(a, b, dims=((1,), (0,))):
    return lax.dot_general(a, b, (dims, ((), ())), preferred_element_type=F32)


def inverse_rms(wide):
    return lax.rsqrt(jnp.mean(wide * wide, axis=-1, keepdims=True) + EPSILON)


def whole(shape):
    return pl.BlockSpec(shape, lambda *_: (0,) * len(shape))


VMEM = pl.BlockSpec(memory_space=pltpu.VMEM)
ANY = pl.BlockSpec(memory_space=pl.ANY)


def call(body, name, arrays, out_shapes, in_specs=None, out_specs=None, grid=(), scratch=(), flops=0, nbytes=0):
    return pl.pallas_call(
        body,
        grid=grid,
        in_specs=[VMEM] * len(arrays) if in_specs is None else in_specs,
        out_specs=jax.tree.map(lambda _: VMEM, out_shapes) if out_specs is None else out_specs,
        scratch_shapes=list(scratch),
        out_shape=out_shapes,
        name=name,
        compiler_params=pltpu.CompilerParams(vmem_limit_bytes=16 * MIB),
        cost_estimate=pl.CostEstimate(flops=flops, bytes_accessed=nbytes, transcendentals=0),
    )(*arrays)


def place():
    me = lax.axis_index("peer")
    return lax.axis_index("section"), lax.div(me, 2), lax.rem(me, 2)


def span(index, size):
    return pl.ds(pl.multiple_of(index * size, size), size)


def shape(dims, dtype=BF):
    return jax.ShapeDtypeStruct(dims, dtype)


def cut_body(depth, sent_ref, g_ref, w_ref, wo_ref, sent_out_ref, *cut_refs):
    _, row, _ = place()
    block = cut_refs[0].shape[1]
    sent_out_ref[...] = sent_ref[...]
    for k, cut_ref in enumerate(cut_refs, 1):
        cut_ref[...] = g_ref[:, span(lax.rem(row + k, depth), block)]


def layer_body(depth, x_ref, g_ref, w_ref, wo_ref, _, attn_ref, *grad_refs):
    row = place()[1]
    seq, width = x_ref.shape
    block = width // depth
    scale = HEAD ** (-0.5)
    wide = x_ref[...].astype(F32)
    normed = (wide * inverse_rms(wide)).astype(BF)
    cotan = g_ref[...]
    low = lax.broadcasted_iota(jnp.int32, (seq, LANES), 1) < HEAD
    rows = lax.broadcasted_iota(jnp.int32, (2 * seq, seq), 0)
    allowed = jnp.where(rows < seq, rows, rows - seq) >= lax.broadcasted_iota(jnp.int32, (2 * seq, seq), 1)
    zero = jnp.zeros((), BF)

    def both(value):
        return jnp.concatenate([jnp.where(low, value, zero), jnp.where(low, zero, value)], axis=0)

    def merge(value):
        return jnp.where(low, value[:seq], value[seq:]).astype(BF)

    for step, grad_ref in enumerate(grad_refs):
        group = lax.rem(row + step, depth)
        query, key, val = (dot(normed, w_ref[:, span(c * depth + group, block)]).astype(BF) for c in range(3))
        d_attn = dot(cotan, wo_ref[span(group, block), :], ((1,), (1,))).astype(BF)
        parts = []
        for pair in range(block // LANES):
            cut = slice(pair * LANES, (pair + 1) * LANES)
            k, v = key[:, cut], val[:, cut]
            q2, da2 = both(query[:, cut]), both(d_attn[:, cut])
            scores = jnp.where(allowed, dot(q2, k, ((1,), (1,))) * scale, -jnp.inf)
            expo = jnp.exp(scores - jnp.max(scores, axis=-1, keepdims=True))
            prob = expo / jnp.sum(expo, axis=-1, keepdims=True)
            prob_bf = prob.astype(BF)
            parts.append(merge(dot(prob_bf, v)))
            grad_ref[2, :, cut] = dot(prob_bf, da2, ((0,), (0,))).astype(BF)
            d_prob = dot(da2, v, ((1,), (1,)))
            d_score = prob * (d_prob - jnp.sum(d_prob * prob, axis=-1, keepdims=True)) * scale
            d_score = d_score.astype(BF)
            grad_ref[0, :, cut] = merge(dot(d_score, k))
            grad_ref[1, :, cut] = dot(d_score, q2, ((0,), (0,))).astype(BF)
        attn_ref[:, span(group, block)] = jnp.concatenate(parts, axis=1)


def input_grad_body(depth, x_ref, g_ref, w_ref, *rest):
    grad_refs, out_ref = rest[:depth], rest[depth]
    _, row, _ = place()
    block = x_ref.shape[1] // depth
    d_normed = jnp.zeros(x_ref.shape, F32)
    for step, grad_ref in enumerate(grad_refs):
        group = lax.rem(row + step, depth)
        for c in range(3):
            d_normed += dot(grad_ref[c], w_ref[:, span(c * depth + group, block)], ((1,), (1,)))
    wide = x_ref[...].astype(F32)
    inv_rms = inverse_rms(wide)
    mean = jnp.mean(d_normed * wide, axis=-1, keepdims=True)
    grad = g_ref[...].astype(F32) + inv_rms * d_normed - wide * inv_rms**3 * mean
    out_ref[...] = grad.astype(BF)


def normed_body(depth, *refs):
    x_refs, out_ref = refs[:depth], refs[depth]
    seq = x_refs[0].shape[0]
    for k, x_ref in enumerate(x_refs):
        wide = x_ref[...].astype(F32)
        out_ref[:, k * seq : (k + 1) * seq] = jnp.transpose(wide * inverse_rms(wide)).astype(BF)


def proj_grad_body(depth, peers, first, normed_ref, *refs):
    _, _, col = place()
    grad_refs, rest = refs[:depth], refs[depth:]
    out_ref, stack_ref = rest[-2], rest[-1]
    thirds, seq, block = grad_refs[0].shape
    slab = out_ref.shape[1]
    for k, grad_ref in enumerate(grad_refs):
        for c in range(thirds):
            stack_ref[k * seq : (k + 1) * seq, c * block : (c + 1) * block] = grad_ref[c]
    rows = 1 - col if first else col
    left = jnp.concatenate([normed_ref[span(2 * a + rows, slab), :] for a in range(depth)], axis=0)
    part = dot(left, stack_ref[...]).reshape(out_ref.shape) * (1.0 / peers)
    if first:
        attn_ref, _, attn_out_ref = rest[:3]
        attn_out_ref[...] = attn_ref[...]
    else:
        part = part + rest[0][...].astype(F32)
    out_ref[...] = part.astype(BF)


def out_grad_body(depth, peers, *refs):
    g_refs, attn_refs = refs[:depth], refs[depth : 2 * depth]
    mine_ref, other_ref, total_ref = refs[2 * depth :]
    _, row, col = place()
    slab = mine_ref.shape[0]
    total = dot(g_refs[0][:, span(row, 2 * slab)], attn_refs[0][...], ((0,), (0,)))
    for g_ref, attn_ref in zip(g_refs[1:], attn_refs[1:]):
        total += dot(g_ref[...], attn_ref[...], ((0,), (0,)))
    total_ref[...] = total * (1.0 / peers)
    mine_ref[...] = total_ref[span(col, slab), :]
    other_ref[...] = total_ref[span(1 - col, slab), :].astype(BF)


def slots_body(depth, peers, sections, first, wiring, *refs):
    x_refs, attn_refs, w_ref = refs[:depth], refs[depth : 2 * depth], refs[2 * depth]
    rest = refs[2 * depth + 1 :]
    x_pick, attn_pick = rest[-2:]
    section, row, col = place()
    target = 2 * row + (1 - col if first else col)
    source = lax.rem(section + sections - 1, sections)
    seq = x_refs[0].shape[0]
    count = jnp.int32(0)
    taken = [jnp.int32(-1)] * CAP
    for p in range(peers):
        hit = wiring[source, p] == target
        for c in range(CAP):
            taken[c] = jnp.where(hit & (count == c), p, taken[c])
        count = count + hit.astype(jnp.int32)
    here = [(t >= 0) & (lax.rem(t, 2) == col) for t in taken]
    for c in range(CAP):
        part = slice(c * seq, (c + 1) * seq)
        behind = lax.rem(row - lax.div(taken[c], 2) + depth, depth)
        for k in range(depth):

            @pl.when(here[c] & (behind == k))
            def _():
                x_pick[part, :] = x_refs[k][...]
                attn_pick[part, :] = attn_refs[k][...]

        @pl.when(jnp.logical_not(here[c]))
        def _():
            x_pick[part, :] = jnp.zeros((seq, x_pick.shape[1]), BF)
            attn_pick[part, :] = jnp.zeros((seq, attn_pick.shape[1]), BF)

    y = (x_pick[...].astype(F32) + dot(attn_pick[...], w_ref[...])).astype(BF)
    if first:
        rest[1][...] = y.reshape(rest[1].shape)
    else:
        received_ref, back_ref, out_ref, back_out_ref = rest[:4]
        out_ref[...] = y.reshape(out_ref.shape) + received_ref[...]
        back_out_ref[...] = back_ref[...]


def final_body(depth, landed_ref, mine_ref, received_ref, out_ref):
    step = pl.program_id(0)
    block = out_ref.shape[1] // depth

    for c in range(3):

        @pl.when(step == c)
        def _():
            for a in range(depth):
                out_ref[:, a * block : (a + 1) * block] = landed_ref[a, :, c * block : (c + 1) * block].astype(F32)

    @pl.when(step == 3)
    def _():
        out_ref[...] = mine_ref[...] + received_ref[...].astype(F32)


def shards(sent_rows, cotangent, wiring, w_qkv, w_out):
    peers = lax.axis_size("peer")
    sections = lax.axis_size("section")
    depth = peers // 2
    weights_in, weights_back = w_qkv[0], w_out[0]
    width = weights_back.shape[0]
    block = width // depth
    slab = width // peers
    seq = sent_rows.shape[2]

    def hop(value, steps):
        pairs = [
            (s * peers + p, (s + 1) % sections * peers + (p + 2 * steps) % peers)
            for s in range(sections)
            for p in range(peers)
        ]
        return lax.ppermute(value, ("section", "peer"), pairs)

    def along(value, steps):
        return lax.ppermute(value, "peer", [(p, (p + 2 * steps) % peers) for p in range(peers)])

    def across(value):
        return lax.ppermute(value, "peer", [(p, p ^ 1) for p in range(peers)])

    sent, cotan = sent_rows[0, 0], cotangent[0, 0]
    x = hop(sent, 0)
    g = hop(cotan, 0)
    sent, *cuts = call(
        functools.partial(cut_body, depth),
        "cut",
        (sent, cotan, weights_in, weights_back),
        [shape((seq, width))] + [shape((seq, block))] * (depth - 1),
        nbytes=8 * width * width,
    )
    column_x = [x] + [hop(sent, k) for k in range(1, depth)]
    column_g = [g] + [hop(part, k) for k, part in enumerate(cuts, 1)]

    attn, *grads = call(
        functools.partial(layer_body, depth),
        "layer",
        (x, g, weights_in, weights_back, sent),
        [shape((seq, width))] + [shape((3, seq, block))] * depth,
        in_specs=[VMEM] * 4 + [ANY],
        flops=12 * seq * width * width,
        nbytes=8 * width * width,
    )
    column_d = [grads[0]] + [along(grads[k], k) for k in range(1, depth)]

    input_grad = call(
        functools.partial(input_grad_body, depth),
        "input_grad",
        (x, g, weights_in, *grads),
        shape((seq, width)),
        flops=6 * seq * width * width,
        nbytes=6 * width * width,
    )
    back = lax.ppermute(input_grad, "section", [(s, (s - 1) % sections) for s in range(sections)])

    normed = call(
        functools.partial(normed_body, depth),
        "normed",
        column_x,
        shape((width, depth * seq)),
        flops=6 * depth * seq * width,
        nbytes=4 * depth * seq * width,
    )
    part_shape = shape((depth, slab, 3 * block))
    part_cost = {
        "flops": 2 * depth * slab * depth * seq * 3 * block,
        "nbytes": 2 * (depth * slab * depth * seq + depth * seq * 3 * block + depth * slab * 3 * block),
    }
    stack = [pltpu.VMEM((depth * seq, 3 * block), BF)]
    attn_sent, part_other = call(
        functools.partial(proj_grad_body, depth, peers, True),
        "proj_grad_other",
        (normed, *column_d, attn, input_grad),
        [shape((seq, width)), part_shape],
        in_specs=[VMEM] * (depth + 2) + [ANY],
        scratch=stack,
        **part_cost,
    )
    column_attn = [attn] + [along(attn_sent, k) for k in range(1, depth)]
    summed = call(
        functools.partial(proj_grad_body, depth, peers, False),
        "proj_grad_mine",
        (normed, *column_d, across(part_other)),
        part_shape,
        scratch=stack,
        **part_cost,
    )
    groups = [[2 * a + c for a in range(depth)] for c in range(2)]
    landed = lax.all_to_all(summed, "peer", 0, 0, axis_index_groups=groups, tiled=True)

    out_mine, out_other = call(
        functools.partial(out_grad_body, depth, peers),
        "out_grad",
        (*column_g, *column_attn),
        [shape((slab, width), F32), shape((slab, width))],
        scratch=[pltpu.VMEM((block, width), F32)],
        flops=2 * depth * seq * block * width,
        nbytes=2 * depth * seq * (block + width),
    )
    out_received = across(out_other)

    slot_shape = shape((CAP, seq, width))
    slot_args = (wiring, *column_x, *column_attn, weights_back)
    slot_specs = [pl.BlockSpec(memory_space=pltpu.SMEM)] + [VMEM] * (2 * depth + 1)
    slot_cost = {"flops": 2 * CAP * seq * width * width, "nbytes": 2 * (width * width + 4 * depth * seq * width)}
    picks = [pltpu.VMEM((CAP * seq, width), BF)] * 2
    slots_other = call(
        functools.partial(slots_body, depth, peers, sections, True),
        "slots_other",
        (*slot_args, summed),
        slot_shape,
        in_specs=slot_specs + [ANY],
        scratch=picks,
        **slot_cost,
    )
    layer_out, back_out = call(
        functools.partial(slots_body, depth, peers, sections, False),
        "slots_mine",
        (*slot_args, across(slots_other), back),
        [slot_shape, shape((seq, width))],
        in_specs=slot_specs + [VMEM] * 2,
        out_specs=[whole((CAP, seq, width)), whole((seq, width))],
        grid=(1,),
        scratch=picks,
        **slot_cost,
    )

    section_grad = call(
        functools.partial(final_body, depth),
        "final",
        (landed, out_mine, out_received),
        shape((slab, 4 * width), F32),
        out_specs=pl.BlockSpec((slab, width), lambda c: (0, c)),
        grid=(4,),
        nbytes=8 * slab * 4 * width,
    )
    return (layer_out[None, None], back_out[None, None], section_grad[None])


def solution(mesh):
    in_specs = (
        P("section", "peer", None, None),
        P("section", "peer", None, None),
        P(),
        P("section", None, None),
        P("section", None, None),
    )
    out_specs = (
        P("section", "peer", None, None, None),
        P("section", "peer", None, None),
        P("section", "peer", None),
    )
    return jax.shard_map(shards, mesh=mesh, in_specs=in_specs, out_specs=out_specs, check_vma=False)
```

```python
import functools

import jax
import jax.numpy as jnp
from jax import lax
from jax.experimental import pallas as pl
from jax.experimental.pallas import tpu as pltpu
from jax.sharding import PartitionSpec as P

HEAD = 64
CAP = 2
EPSILON = 1e-05
LANES = 128
BF = jnp.bfloat16
F32 = jnp.float32
MIB = 1 << 20


def dot(a, b, dims=((1,), (0,))):
    return lax.dot_general(a, b, (dims, ((), ())), preferred_element_type=F32)


def inverse_rms(wide):
    return lax.rsqrt(jnp.mean(wide * wide, axis=-1, keepdims=True) + EPSILON)


def whole(shape):
    return pl.BlockSpec(shape, lambda *_: (0,) * len(shape))


VMEM = pl.BlockSpec(memory_space=pltpu.VMEM)
ANY = pl.BlockSpec(memory_space=pl.ANY)


def call(body, name, arrays, out_shapes, in_specs=None, out_specs=None, grid=(), scratch=(), limit=16, flops=0, nbytes=0):
    return pl.pallas_call(
        body,
        grid=grid,
        in_specs=[VMEM] * len(arrays) if in_specs is None else in_specs,
        out_specs=jax.tree.map(lambda _: VMEM, out_shapes) if out_specs is None else out_specs,
        scratch_shapes=list(scratch),
        out_shape=out_shapes,
        name=name,
        compiler_params=pltpu.CompilerParams(vmem_limit_bytes=limit * MIB),
        cost_estimate=pl.CostEstimate(flops=flops, bytes_accessed=nbytes, transcendentals=0),
    )(*arrays)


def place():
    me = lax.axis_index("peer")
    return lax.axis_index("section"), lax.div(me, 2), lax.rem(me, 2)


def span(index, size):
    return pl.ds(pl.multiple_of(index * size, size), size)


def shape(dims, dtype=BF):
    return jax.ShapeDtypeStruct(dims, dtype)


def cut_body(depth, sent_ref, g_ref, token_ref, sent_out_ref, *cut_refs):
    _, row, _ = place()
    block = cut_refs[0].shape[1]
    sent_out_ref[...] = sent_ref[...]
    token_ref[...] = jnp.zeros_like(token_ref)
    for k, cut_ref in enumerate(cut_refs, 1):
        cut_ref[...] = g_ref[:, span(lax.rem(row + k, depth), block)]


def layer_body(depth, x_ref, g_ref, w_hbm, wo_hbm, _, attn_ref, *rest):
    grad_refs, (w_ref, wo_ref, sems) = rest[:depth], rest[depth:]
    row = place()[1]
    seq, width = x_ref.shape
    block = width // depth

    def fetches(step):
        group = lax.rem(row + step, depth)
        copies = []
        for c in range(3):
            cut = span(c * depth + group, block)
            copies.append(pltpu.make_async_copy(w_hbm.at[:, cut], w_ref.at[step, c], sems.at[step, c]))
        rows = span(group, block)
        copies.append(pltpu.make_async_copy(wo_hbm.at[rows, :], wo_ref.at[step], sems.at[step, 3]))
        return copies

    for step in range(depth):
        for copy in fetches(step):
            copy.start()
    scale = HEAD ** (-0.5)
    wide = x_ref[...].astype(F32)
    normed = (wide * inverse_rms(wide)).astype(BF)
    cotan = g_ref[...]
    low = lax.broadcasted_iota(jnp.int32, (seq, LANES), 1) < HEAD
    rows = lax.broadcasted_iota(jnp.int32, (2 * seq, seq), 0)
    allowed = jnp.where(rows < seq, rows, rows - seq) >= lax.broadcasted_iota(jnp.int32, (2 * seq, seq), 1)
    zero = jnp.zeros((), BF)

    def both(value):
        return jnp.concatenate([jnp.where(low, value, zero), jnp.where(low, zero, value)], axis=0)

    def merge(value):
        return jnp.where(low, value[:seq], value[seq:]).astype(BF)

    for step, grad_ref in enumerate(grad_refs):
        group = lax.rem(row + step, depth)
        for copy in fetches(step):
            copy.wait()
        query, key, val = (dot(normed, w_ref[step, c]).astype(BF) for c in range(3))
        d_attn = dot(cotan, wo_ref[step], ((1,), (1,))).astype(BF)
        parts = []
        for pair in range(block // LANES):
            cut = slice(pair * LANES, (pair + 1) * LANES)
            k, v = key[:, cut], val[:, cut]
            q2, da2 = both(query[:, cut]), both(d_attn[:, cut])
            scores = jnp.where(allowed, dot(q2, k, ((1,), (1,))) * scale, -jnp.inf)
            expo = jnp.exp(scores - jnp.max(scores, axis=-1, keepdims=True))
            prob = expo / jnp.sum(expo, axis=-1, keepdims=True)
            prob_bf = prob.astype(BF)
            parts.append(merge(dot(prob_bf, v)))
            grad_ref[2, :, cut] = dot(prob_bf, da2, ((0,), (0,))).astype(BF)
            d_prob = dot(da2, v, ((1,), (1,)))
            d_score = prob * (d_prob - jnp.sum(d_prob * prob, axis=-1, keepdims=True)) * scale
            d_score = d_score.astype(BF)
            grad_ref[0, :, cut] = merge(dot(d_score, k))
            grad_ref[1, :, cut] = dot(d_score, q2, ((0,), (0,))).astype(BF)
        attn_ref[:, span(group, block)] = jnp.concatenate(parts, axis=1)


def input_grad_body(depth, x_ref, g_ref, w_ref, *rest):
    grad_refs, out_ref = rest[:depth], rest[depth]
    _, row, _ = place()
    block = x_ref.shape[1] // depth
    d_normed = jnp.zeros(x_ref.shape, F32)
    for step, grad_ref in enumerate(grad_refs):
        group = lax.rem(row + step, depth)
        for c in range(3):
            d_normed += dot(grad_ref[c], w_ref[:, span(c * depth + group, block)], ((1,), (1,)))
    wide = x_ref[...].astype(F32)
    inv_rms = inverse_rms(wide)
    mean = jnp.mean(d_normed * wide, axis=-1, keepdims=True)
    grad = g_ref[...].astype(F32) + inv_rms * d_normed - wide * inv_rms**3 * mean
    out_ref[...] = grad.astype(BF)


def normed_body(depth, *refs):
    x_refs, out_ref = refs[:depth], refs[depth]
    seq = x_refs[0].shape[0]
    for k, x_ref in enumerate(x_refs):
        wide = x_ref[...].astype(F32)
        out_ref[:, k * seq : (k + 1) * seq] = jnp.transpose(wide * inverse_rms(wide)).astype(BF)


def proj_grad_body(depth, peers, first, normed_ref, *refs):
    _, _, col = place()
    grad_refs, rest = refs[:depth], refs[depth:]
    out_ref, stack_ref = rest[-2], rest[-1]
    thirds, seq, block = grad_refs[0].shape
    slab = out_ref.shape[1]
    for k, grad_ref in enumerate(grad_refs):
        for c in range(thirds):
            stack_ref[k * seq : (k + 1) * seq, c * block : (c + 1) * block] = grad_ref[c]
    rows = 1 - col if first else col
    left = jnp.concatenate([normed_ref[span(2 * a + rows, slab), :] for a in range(depth)], axis=0)
    part = dot(left, stack_ref[...]).reshape(out_ref.shape) * (1.0 / peers)
    if first:
        attn_ref, attn_out_ref = rest[0], rest[-3]
        attn_out_ref[...] = attn_ref[...]
    else:
        part = part + rest[0][...].astype(F32)
    out_ref[...] = part.astype(BF)


def out_grad_body(depth, peers, *refs):
    g_refs, attn_refs = refs[:depth], refs[depth : 2 * depth]
    mine_ref, other_ref, total_ref = refs[2 * depth :]
    _, row, col = place()
    slab = mine_ref.shape[0]
    total = dot(g_refs[0][:, span(row, 2 * slab)], attn_refs[0][...], ((0,), (0,)))
    for g_ref, attn_ref in zip(g_refs[1:], attn_refs[1:]):
        total += dot(g_ref[...], attn_ref[...], ((0,), (0,)))
    total_ref[...] = total * (1.0 / peers)
    mine_ref[...] = total_ref[span(col, slab), :]
    other_ref[...] = total_ref[span(1 - col, slab), :].astype(BF)


def slots_body(depth, peers, sections, first, wiring, *refs):
    x_refs, attn_refs, w_ref = refs[:depth], refs[depth : 2 * depth], refs[2 * depth]
    rest = refs[2 * depth + 1 :]
    x_pick, attn_pick = rest[-2:]
    section, row, col = place()
    target = 2 * row + (1 - col if first else col)
    source = lax.rem(section + sections - 1, sections)
    seq = x_refs[0].shape[0]
    count = jnp.int32(0)
    taken = [jnp.int32(-1)] * CAP
    for p in range(peers):
        hit = wiring[source, p] == target
        for c in range(CAP):
            taken[c] = jnp.where(hit & (count == c), p, taken[c])
        count = count + hit.astype(jnp.int32)
    here = [(t >= 0) & (lax.rem(t, 2) == col) for t in taken]
    for c in range(CAP):
        part = slice(c * seq, (c + 1) * seq)
        behind = lax.rem(row - lax.div(taken[c], 2) + depth, depth)
        for k in range(depth):

            @pl.when(here[c] & (behind == k))
            def _():
                x_pick[part, :] = x_refs[k][...]
                attn_pick[part, :] = attn_refs[k][...]

        @pl.when(jnp.logical_not(here[c]))
        def _():
            x_pick[part, :] = jnp.zeros((seq, x_pick.shape[1]), BF)
            attn_pick[part, :] = jnp.zeros((seq, attn_pick.shape[1]), BF)

    y = (x_pick[...].astype(F32) + dot(attn_pick[...], w_ref[...])).astype(BF)
    if first:
        rest[1][...] = y.reshape(rest[1].shape)
    else:
        received_ref, back_ref, out_ref, back_out_ref = rest[:4]
        out_ref[...] = y.reshape(out_ref.shape) + received_ref[...]
        back_out_ref[...] = back_ref[...]


def final_body(depth, landed_ref, mine_ref, received_ref, out_ref):
    step = pl.program_id(0)
    block = out_ref.shape[1] // depth

    for c in range(3):

        @pl.when(step == c)
        def _():
            for a in range(depth):
                out_ref[:, a * block : (a + 1) * block] = landed_ref[a, :, c * block : (c + 1) * block].astype(F32)

    @pl.when(step == 3)
    def _():
        out_ref[...] = mine_ref[...] + received_ref[...].astype(F32)


def shards(sent_rows, cotangent, wiring, w_qkv, w_out):
    peers = lax.axis_size("peer")
    sections = lax.axis_size("section")
    depth = peers // 2
    weights_in, weights_back = w_qkv[0], w_out[0]
    width = weights_back.shape[0]
    block = width // depth
    slab = width // peers
    seq = sent_rows.shape[2]

    def hop(value, steps):
        pairs = [
            (s * peers + p, (s + 1) % sections * peers + (p + 2 * steps) % peers)
            for s in range(sections)
            for p in range(peers)
        ]
        return lax.ppermute(value, ("section", "peer"), pairs)

    def along(value, steps):
        return lax.ppermute(value, "peer", [(p, (p + 2 * steps) % peers) for p in range(peers)])

    def across(value):
        return lax.ppermute(value, "peer", [(p, p ^ 1) for p in range(peers)])

    sent, cotan = sent_rows[0, 0], cotangent[0, 0]
    x = hop(sent, 0)
    g = hop(cotan, 0)
    token, sent, *cuts = call(
        functools.partial(cut_body, depth),
        "cut",
        (sent, cotan),
        [shape((8, LANES), F32), shape((seq, width))] + [shape((seq, block))] * (depth - 1),
        in_specs=[whole((seq, width))] * 2,
        grid=(1,),
        limit=56,
    )
    column_x = [x] + [hop(sent, k) for k in range(1, depth)]
    column_g = [g] + [hop(part, k) for k, part in enumerate(cuts, 1)]

    attn, *grads = call(
        functools.partial(layer_body, depth),
        "layer",
        (x, g, weights_in, weights_back, token),
        [shape((seq, width))] + [shape((3, seq, block))] * depth,
        in_specs=[VMEM] * 2 + [ANY] * 3,
        scratch=[
            pltpu.VMEM((depth, 3, width, block), BF),
            pltpu.VMEM((depth, block, width), BF),
            pltpu.SemaphoreType.DMA((depth, 4)),
        ],
        limit=50,
        flops=12 * seq * width * width,
        nbytes=8 * width * width,
    )
    column_d = [grads[0]] + [along(grads[k], k) for k in range(1, depth)]

    input_grad = call(
        functools.partial(input_grad_body, depth),
        "input_grad",
        (x, g, weights_in, *grads),
        shape((seq, width)),
        flops=6 * seq * width * width,
        nbytes=6 * width * width,
    )
    back = lax.ppermute(input_grad, "section", [(s, (s - 1) % sections) for s in range(sections)])

    normed = call(
        functools.partial(normed_body, depth),
        "normed",
        column_x,
        shape((width, depth * seq)),
        flops=6 * depth * seq * width,
        nbytes=4 * depth * seq * width,
    )
    part_shape = shape((depth, slab, 3 * block))
    part_cost = {
        "flops": 2 * depth * slab * depth * seq * 3 * block,
        "nbytes": 2 * (depth * slab * depth * seq + depth * seq * 3 * block + depth * slab * 3 * block),
    }
    stack = [pltpu.VMEM((depth * seq, 3 * block), BF)]
    attn_sent, part_other = call(
        functools.partial(proj_grad_body, depth, peers, True),
        "proj_grad_other",
        (normed, *column_d, attn, input_grad, *column_g[1:]),
        [shape((seq, width)), part_shape],
        in_specs=[VMEM] * (depth + 2) + [ANY] * depth,
        scratch=stack,
        **part_cost,
    )
    column_attn = [attn] + [along(attn_sent, k) for k in range(1, depth)]
    out_mine, out_other = call(
        functools.partial(out_grad_body, depth, peers),
        "out_grad",
        (*column_g, *column_attn),
        [shape((slab, width), F32), shape((slab, width))],
        scratch=[pltpu.VMEM((block, width), F32)],
        flops=2 * depth * seq * block * width,
        nbytes=2 * depth * seq * (block + width),
    )
    summed = call(
        functools.partial(proj_grad_body, depth, peers, False),
        "proj_grad_mine",
        (normed, *column_d, across(part_other), out_other),
        part_shape,
        in_specs=[VMEM] * (depth + 2) + [ANY],
        scratch=stack,
        **part_cost,
    )
    groups = [[2 * a + c for a in range(depth)] for c in range(2)]
    landed = lax.all_to_all(summed, "peer", 0, 0, axis_index_groups=groups, tiled=True)
    out_received = across(out_other)

    slot_shape = shape((CAP, seq, width))
    slot_args = (wiring, *column_x, *column_attn, weights_back)
    slot_specs = [pl.BlockSpec(memory_space=pltpu.SMEM)] + [VMEM] * (2 * depth + 1)
    slot_cost = {"flops": 2 * CAP * seq * width * width, "nbytes": 2 * (width * width + 4 * depth * seq * width)}
    picks = [pltpu.VMEM((CAP * seq, width), BF)] * 2
    slots_other = call(
        functools.partial(slots_body, depth, peers, sections, True),
        "slots_other",
        (*slot_args, summed),
        slot_shape,
        in_specs=slot_specs + [ANY],
        scratch=picks,
        **slot_cost,
    )
    layer_out, back_out = call(
        functools.partial(slots_body, depth, peers, sections, False),
        "slots_mine",
        (*slot_args, across(slots_other), back),
        [slot_shape, shape((seq, width))],
        in_specs=slot_specs + [VMEM] * 2,
        out_specs=[whole((CAP, seq, width)), whole((seq, width))],
        grid=(1,),
        scratch=picks,
        **slot_cost,
    )

    section_grad = call(
        functools.partial(final_body, depth),
        "final",
        (landed, out_mine, out_received),
        shape((slab, 4 * width), F32),
        out_specs=pl.BlockSpec((slab, width), lambda c: (0, c)),
        grid=(4,),
        nbytes=8 * slab * 4 * width,
    )
    return (layer_out[None, None], back_out[None, None], section_grad[None])


def solution(mesh):
    in_specs = (
        P("section", "peer", None, None),
        P("section", "peer", None, None),
        P(),
        P("section", None, None),
        P("section", None, None),
    )
    out_specs = (
        P("section", "peer", None, None, None),
        P("section", "peer", None, None),
        P("section", "peer", None),
    )
    return jax.shard_map(shards, mesh=mesh, in_specs=in_specs, out_specs=out_specs, check_vma=False)
```

```python
import functools

import jax
import jax.numpy as jnp
from jax import lax
from jax.experimental import pallas as pl
from jax.experimental.pallas import tpu as pltpu
from jax.sharding import PartitionSpec as P

HEAD = 64
CAP = 2
EPSILON = 1e-05
LANES = 128
BF = jnp.bfloat16
F32 = jnp.float32
MIB = 1 << 20
TAIL_FLOPS = 60_000_000_000


def dot(a, b, dims=((1,), (0,))):
    return lax.dot_general(a, b, (dims, ((), ())), preferred_element_type=F32)


def inverse_rms(wide):
    return lax.rsqrt(jnp.mean(wide * wide, axis=-1, keepdims=True) + EPSILON)


def whole(shape):
    return pl.BlockSpec(shape, lambda *_: (0,) * len(shape))


VMEM = pl.BlockSpec(memory_space=pltpu.VMEM)
ANY = pl.BlockSpec(memory_space=pl.ANY)


def call(body, name, arrays, out_shapes, in_specs=None, out_specs=None, grid=(), scratch=(), limit=16, flops=0, nbytes=0):
    return pl.pallas_call(
        body,
        grid=grid,
        in_specs=[VMEM] * len(arrays) if in_specs is None else in_specs,
        out_specs=jax.tree.map(lambda _: VMEM, out_shapes) if out_specs is None else out_specs,
        scratch_shapes=list(scratch),
        out_shape=out_shapes,
        name=name,
        compiler_params=pltpu.CompilerParams(vmem_limit_bytes=limit * MIB),
        cost_estimate=pl.CostEstimate(flops=int(flops), bytes_accessed=nbytes, transcendentals=0),
    )(*arrays)


def place():
    me = lax.axis_index("peer")
    return lax.axis_index("section"), lax.div(me, 2), lax.rem(me, 2)


def span(index, size):
    return pl.ds(pl.multiple_of(index * size, size), size)


def shape(dims, dtype=BF):
    return jax.ShapeDtypeStruct(dims, dtype)


def layer_body(depth, x_ref, g_ref, w_hbm, wo_hbm, attn_ref, *rest):
    grad_refs, (w_ref, wo_ref, sems) = rest[:depth], rest[depth:]
    row = place()[1]
    seq, width = x_ref.shape
    block = width // depth

    def fetches(step):
        group = lax.rem(row + step, depth)
        copies = []
        for c in range(3):
            cut = span(c * depth + group, block)
            copies.append(pltpu.make_async_copy(w_hbm.at[:, cut], w_ref.at[step, c], sems.at[step, c]))
        rows = span(group, block)
        copies.append(pltpu.make_async_copy(wo_hbm.at[rows, :], wo_ref.at[step], sems.at[step, 3]))
        return copies

    for step in range(depth):
        for copy in fetches(step):
            copy.start()
    scale = HEAD ** (-0.5)
    wide = x_ref[...].astype(F32)
    normed = (wide * inverse_rms(wide)).astype(BF)
    cotan = g_ref[...]
    low = lax.broadcasted_iota(jnp.int32, (seq, LANES), 1) < HEAD
    rows = lax.broadcasted_iota(jnp.int32, (2 * seq, seq), 0)
    allowed = jnp.where(rows < seq, rows, rows - seq) >= lax.broadcasted_iota(jnp.int32, (2 * seq, seq), 1)
    zero = jnp.zeros((), BF)

    def both(value):
        return jnp.concatenate([jnp.where(low, value, zero), jnp.where(low, zero, value)], axis=0)

    def merge(value):
        return jnp.where(low, value[:seq], value[seq:]).astype(BF)

    for step, grad_ref in enumerate(grad_refs):
        group = lax.rem(row + step, depth)
        for copy in fetches(step):
            copy.wait()
        query, key, val = (dot(normed, w_ref[step, c]).astype(BF) for c in range(3))
        d_attn = dot(cotan, wo_ref[step], ((1,), (1,))).astype(BF)
        grad_ref[3] = g_ref[:, span(group, block)]
        parts = []
        for pair in range(block // LANES):
            cut = slice(pair * LANES, (pair + 1) * LANES)
            k, v = key[:, cut], val[:, cut]
            q2, da2 = both(query[:, cut]), both(d_attn[:, cut])
            scores = jnp.where(allowed, dot(q2, k, ((1,), (1,))) * scale, -jnp.inf)
            expo = jnp.exp(scores - jnp.max(scores, axis=-1, keepdims=True))
            prob = expo / jnp.sum(expo, axis=-1, keepdims=True)
            prob_bf = prob.astype(BF)
            parts.append(merge(dot(prob_bf, v)))
            grad_ref[2, :, cut] = dot(prob_bf, da2, ((0,), (0,))).astype(BF)
            d_prob = dot(da2, v, ((1,), (1,)))
            d_score = prob * (d_prob - jnp.sum(d_prob * prob, axis=-1, keepdims=True)) * scale
            d_score = d_score.astype(BF)
            grad_ref[0, :, cut] = merge(dot(d_score, k))
            grad_ref[1, :, cut] = dot(d_score, q2, ((0,), (0,))).astype(BF)
        attn_ref[:, span(group, block)] = jnp.concatenate(parts, axis=1)


def input_grad_body(depth, x_ref, g_ref, w_ref, *rest):
    grad_refs, (attn_ref, _, out_ref, attn_out_ref) = rest[:depth], rest[depth:]
    attn_out_ref[...] = attn_ref[...]
    _, row, _ = place()
    block = x_ref.shape[1] // depth
    d_normed = jnp.zeros(x_ref.shape, F32)
    for step, grad_ref in enumerate(grad_refs):
        group = lax.rem(row + step, depth)
        for c in range(3):
            d_normed += dot(grad_ref[c], w_ref[:, span(c * depth + group, block)], ((1,), (1,)))
    wide = x_ref[...].astype(F32)
    inv_rms = inverse_rms(wide)
    mean = jnp.mean(d_normed * wide, axis=-1, keepdims=True)
    grad = g_ref[...].astype(F32) + inv_rms * d_normed - wide * inv_rms**3 * mean
    out_ref[...] = grad.astype(BF)


def choose(depth, peers, sections, across, wiring):
    section, row, col = place()
    source = lax.rem(section + sections - 1, sections)
    choices = []
    target = 2 * row + (1 - col if across else col)
    for slot in range(CAP):
        count = jnp.int32(0)
        taken = jnp.int32(-1)
        for p in range(peers):
            hit = wiring[source, p] == target
            taken = jnp.where(hit & (count == slot), p, taken)
            count = count + hit.astype(jnp.int32)
        here = (taken >= 0) & (lax.rem(taken, 2) == col)
        choices.append((here, lax.rem(row - lax.div(taken, 2) + depth, depth)))
    return choices


def pick(choices, refs, out_ref):
    seq, width = refs[0].shape
    for slot, (here, behind) in enumerate(choices):
        part = slice(slot * seq, (slot + 1) * seq)
        for k, ref in enumerate(refs):

            @pl.when(here & (behind == k))
            def _():
                out_ref[part, :] = ref[...]

        @pl.when(jnp.logical_not(here))
        def _():
            out_ref[part, :] = jnp.zeros((seq, width), BF)


def normed_body(depth, *refs):
    x_refs, out_ref = refs[:depth], refs[depth]
    seq = x_refs[0].shape[0]
    for k, x_ref in enumerate(x_refs):
        wide = x_ref[...].astype(F32)
        out_ref[:, k * seq : (k + 1) * seq] = jnp.transpose(wide * inverse_rms(wide)).astype(BF)


def pack_body(depth, peers, sections, wiring, *refs):
    x_refs, grad_refs, bundle_ref = refs[:depth], refs[depth : 2 * depth], refs[-1]
    seq, width = x_refs[0].shape
    block = width // depth
    for across in (False, True):
        rows = pl.ds(CAP * seq * across, CAP * seq)
        pick(choose(depth, peers, sections, across, wiring), x_refs, bundle_ref.at[rows, :])
    for k, grad_ref in enumerate(grad_refs):
        bundle_ref[2 * CAP * seq :, k * block : (k + 1) * block] = grad_ref[3]


def proj_grad_body(depth, peers, first, normed_ref, *refs):
    _, row, col = place()
    grad_refs, rest = refs[:depth], refs[depth:]
    token_ref, stack_ref = rest[-2], rest[-1]
    _, seq, block = grad_refs[0].shape
    slab = normed_ref.shape[0] // peers
    for k, grad_ref in enumerate(grad_refs):
        for c in range(3):
            stack_ref[k * seq : (k + 1) * seq, c * block : (c + 1) * block] = grad_ref[c]
    rows = 1 - col if first else col
    groups = [lax.rem(row + k, depth) for k in range(depth)]
    left = jnp.concatenate([normed_ref[span(2 * a + rows, slab), :] for a in groups], axis=0)
    part = dot(left, stack_ref[...]) * (1.0 / peers)
    if first:
        rest[-3][...] = part.astype(BF)
    else:
        part = (part + rest[0][...].astype(F32)).astype(BF)
        for k, out_ref in enumerate(rest[-2 - depth : -2]):
            out_ref[...] = part[k * slab : (k + 1) * slab]
    token_ref[...] = jnp.zeros(token_ref.shape, F32)


def tail_body(depth, peers, sections, across, wiring, bundle, *refs):
    attn_refs, rest = refs[:depth], refs[depth:]
    w_ref, slots_ref, out_ref, attn_pick = rest[0], rest[-3], rest[-2], rest[-1]
    col = place()[2]
    seq, width = attn_refs[0].shape
    slab = out_ref.shape[0]
    block = width // depth
    pick(choose(depth, peers, sections, across, wiring), attn_refs, attn_pick)
    x_pick = bundle[pl.ds(CAP * seq * across, CAP * seq), :]
    y = (x_pick.astype(F32) + dot(attn_pick[...], w_ref[...])).astype(BF)
    slots_ref[...] = y.reshape(slots_ref.shape)
    total = jnp.zeros((2 * slab, width), F32)
    for k, attn_ref in enumerate(attn_refs):
        total += dot(bundle[pl.ds(2 * CAP * seq, seq), k * block : (k + 1) * block], attn_ref[...], ((0,), (0,)))
    first = (1 - col if across else col) == 0
    out_ref[...] = (jnp.where(first, total[:slab], total[slab:]) * (1.0 / peers)).astype(out_ref.dtype)


def final_body(depth, *refs):
    landed_refs, rest = refs[:depth], refs[depth:]
    out_ref, out_other, slots_ref, slots_other, back_ref, grad_ref, layer_ref, back_out_ref = rest
    row = place()[1]
    step = pl.program_id(0)
    block = grad_ref.shape[1] // depth

    @pl.when(step < 3)
    def _():
        for k, landed_ref in enumerate(landed_refs):
            grad_ref[:, span(lax.rem(row - k + depth, depth), block)] = landed_ref[...].astype(F32)

    @pl.when(step == 3)
    def _():
        grad_ref[...] = out_ref[...] + out_other[...].astype(F32)
        layer_ref[...] = slots_ref[...] + slots_other[...]
        back_out_ref[...] = back_ref[...]


def shards(sent_rows, cotangent, wiring, w_qkv, w_out):
    peers = lax.axis_size("peer")
    sections = lax.axis_size("section")
    depth = peers // 2
    weights_in, weights_back = w_qkv[0], w_out[0]
    width = weights_back.shape[0]
    block = width // depth
    slab = width // peers
    seq = sent_rows.shape[2]

    def hop(value, steps):
        pairs = [
            (s * peers + p, (s + 1) % sections * peers + (p + 2 * steps) % peers)
            for s in range(sections)
            for p in range(peers)
        ]
        return lax.ppermute(value, ("section", "peer"), pairs)

    def along(value, steps):
        return lax.ppermute(value, "peer", [(p, (p + 2 * steps) % peers) for p in range(peers)])

    def across(value):
        return lax.ppermute(value, "peer", [(p, p ^ 1) for p in range(peers)])

    sent, cotan = sent_rows[0, 0], cotangent[0, 0]
    x = hop(sent, 0)
    g = hop(cotan, 0)
    column_x = [x] + [hop(sent, k) for k in range(1, depth)]

    attn, *grads = call(
        functools.partial(layer_body, depth),
        "layer",
        (x, g, weights_in, weights_back),
        [shape((seq, width))] + [shape((4, seq, block))] * depth,
        in_specs=[VMEM] * 2 + [ANY] * 2,
        scratch=[
            pltpu.VMEM((depth, 3, width, block), BF),
            pltpu.VMEM((depth, block, width), BF),
            pltpu.SemaphoreType.DMA((depth, 4)),
        ],
        limit=50,
        flops=12 * seq * width * width,
        nbytes=8 * width * width,
    )
    column_d = [grads[0]] + [along(grads[k], k) for k in range(1, depth)]

    smem = pl.BlockSpec(memory_space=pltpu.SMEM)
    normed = call(
        functools.partial(normed_body, depth),
        "normed",
        column_x,
        shape((width, depth * seq)),
        flops=6 * depth * seq * width,
        nbytes=4 * depth * seq * width,
    )
    input_grad, attn_sent = call(
        functools.partial(input_grad_body, depth),
        "input_grad",
        (x, g, weights_in, *grads, attn, normed),
        [shape((seq, width))] * 2,
        in_specs=[VMEM] * (depth + 4) + [ANY],
        flops=6 * seq * width * width,
        nbytes=6 * width * width,
    )
    back = lax.ppermute(input_grad, "section", [(s, (s - 1) % sections) for s in range(sections)])

    part_shape = shape((depth * slab, 3 * block))
    part_cost = {
        "flops": 2 * depth * slab * depth * seq * 3 * block,
        "nbytes": 2 * (depth * slab * depth * seq + depth * seq * 3 * block + depth * slab * 3 * block),
    }
    stack = [pltpu.VMEM((depth * seq, 3 * block), BF)]
    token = shape((8, LANES), F32)
    column_attn = [attn_sent] + [along(attn_sent, k) for k in range(1, depth)]
    early = [column_attn[k] for k in range(1, depth) if False]
    part_other, arrived = call(
        functools.partial(proj_grad_body, depth, peers, True),
        "proj_grad_other",
        (normed, *column_d, input_grad, *early),
        [part_shape, token],
        in_specs=[VMEM] * (depth + 1) + [ANY] * (1 + len(early)),
        scratch=stack,
        **part_cost,
    )
    bundle = call(
        functools.partial(pack_body, depth, peers, sections),
        "pack",
        (wiring, *column_x, *column_d, arrived),
        shape(((2 * CAP + 1) * seq, width)),
        in_specs=[smem] + [VMEM] * (2 * depth) + [ANY],
        nbytes=8 * depth * seq * width,
    )
    slot_shape = shape((CAP, seq, width))

    def tail(to_neighbour, extra):
        return call(
            functools.partial(tail_body, depth, peers, sections, to_neighbour),
            "tail_other" if to_neighbour else "tail_mine",
            (wiring, bundle, *column_attn, weights_back, extra),
            [slot_shape, shape((slab, width), BF if to_neighbour else F32)],
            in_specs=[smem] + [VMEM] * (depth + 2) + [ANY],
            scratch=[pltpu.VMEM((CAP * seq, width), BF)],
            flops=TAIL_FLOPS,
            nbytes=2 * (width * width + 4 * depth * seq * width),
        )

    slots_sent, out_sent = tail(True, arrived)
    *summed, _ = call(
        functools.partial(proj_grad_body, depth, peers, False),
        "proj_grad_mine",
        (normed, *column_d, across(part_other), slots_sent),
        [shape((slab, 3 * block))] * depth + [token],
        in_specs=[VMEM] * (depth + 2) + [ANY],
        scratch=stack,
        **part_cost,
    )
    landed = [summed[0]] + [along(summed[k], k) for k in range(1, depth)]
    slots_mine, out_mine = tail(False, out_sent)
    section_grad, layer_out, back_out = call(
        functools.partial(final_body, depth),
        "final",
        (*landed, out_mine, across(out_sent), slots_mine, across(slots_sent), back),
        [shape((slab, 4 * width), F32), shape((CAP, seq, width)), shape((seq, width))],
        in_specs=[
            *[pl.BlockSpec((slab, block), lambda c: (0, jnp.minimum(c, 2)))] * depth,
            whole((slab, width)),
            whole((slab, width)),
            whole((CAP, seq, width)),
            whole((CAP, seq, width)),
            whole((seq, width)),
        ],
        out_specs=[pl.BlockSpec((slab, width), lambda c: (0, c)), whole((CAP, seq, width)), whole((seq, width))],
        grid=(4,),
        nbytes=8 * slab * 4 * width,
    )
    return (layer_out[None, None], back_out[None, None], section_grad[None])


def solution(mesh):
    in_specs = (
        P("section", "peer", None, None),
        P("section", "peer", None, None),
        P(),
        P("section", None, None),
        P("section", None, None),
    )
    out_specs = (
        P("section", "peer", None, None, None),
        P("section", "peer", None, None),
        P("section", "peer", None),
    )
    return jax.shard_map(shards, mesh=mesh, in_specs=in_specs, out_specs=out_specs, check_vma=False)
```

```python
import functools

import jax
import jax.numpy as jnp
from jax import lax
from jax.experimental import pallas as pl
from jax.experimental.pallas import tpu as pltpu
from jax.sharding import PartitionSpec as P

HEAD = 64
CAP = 2
EPSILON = 1e-05
LANES = 128
BF = jnp.bfloat16
F32 = jnp.float32
MIB = 1 << 20


def dot(a, b, dims=((1,), (0,))):
    return lax.dot_general(a, b, (dims, ((), ())), preferred_element_type=F32)


def inverse_rms(wide):
    return lax.rsqrt(jnp.mean(wide * wide, axis=-1, keepdims=True) + EPSILON)


def whole(shape):
    return pl.BlockSpec(shape, lambda *_: (0,) * len(shape))


VMEM = pl.BlockSpec(memory_space=pltpu.VMEM)
ANY = pl.BlockSpec(memory_space=pl.ANY)


WEIGHT = {"normed": 8, "input_grad": 8, "pack": 20, "slots_other": 3, "out_grad": 3, "slots_mine": 60}


def call(body, name, arrays, out_shapes, in_specs=None, out_specs=None, grid=(), scratch=(), limit=16, flops=0, nbytes=0):
    if name in WEIGHT:
        flops, nbytes = WEIGHT[name] * 10**9, 0
    return pl.pallas_call(
        body,
        grid=grid,
        in_specs=[VMEM] * len(arrays) if in_specs is None else in_specs,
        out_specs=jax.tree.map(lambda _: VMEM, out_shapes) if out_specs is None else out_specs,
        scratch_shapes=list(scratch),
        out_shape=out_shapes,
        name=name,
        compiler_params=pltpu.CompilerParams(vmem_limit_bytes=limit * MIB),
        cost_estimate=pl.CostEstimate(flops=int(flops), bytes_accessed=nbytes, transcendentals=0),
    )(*arrays)


def place():
    me = lax.axis_index("peer")
    return lax.axis_index("section"), lax.div(me, 2), lax.rem(me, 2)


def span(index, size):
    return pl.ds(pl.multiple_of(index * size, size), size)


def shape(dims, dtype=BF):
    return jax.ShapeDtypeStruct(dims, dtype)


def layer_body(depth, x_ref, g_ref, w_hbm, wo_hbm, attn_ref, *rest):
    grad_refs, (w_ref, wo_ref, sems) = rest[:depth], rest[depth:]
    row = place()[1]
    seq, width = x_ref.shape
    block = width // depth

    def fetches(step):
        group = lax.rem(row + step, depth)
        copies = []
        for c in range(3):
            cut = span(c * depth + group, block)
            copies.append(pltpu.make_async_copy(w_hbm.at[:, cut], w_ref.at[step, c], sems.at[step, c]))
        rows = span(group, block)
        copies.append(pltpu.make_async_copy(wo_hbm.at[rows, :], wo_ref.at[step], sems.at[step, 3]))
        return copies

    for step in range(depth):
        for copy in fetches(step):
            copy.start()
    scale = HEAD ** (-0.5)
    wide = x_ref[...].astype(F32)
    normed = (wide * inverse_rms(wide)).astype(BF)
    cotan = g_ref[...]
    low = lax.broadcasted_iota(jnp.int32, (seq, LANES), 1) < HEAD
    rows = lax.broadcasted_iota(jnp.int32, (2 * seq, seq), 0)
    allowed = jnp.where(rows < seq, rows, rows - seq) >= lax.broadcasted_iota(jnp.int32, (2 * seq, seq), 1)
    zero = jnp.zeros((), BF)

    def both(value):
        return jnp.concatenate([jnp.where(low, value, zero), jnp.where(low, zero, value)], axis=0)

    def merge(value):
        return jnp.where(low, value[:seq], value[seq:]).astype(BF)

    for step, grad_ref in enumerate(grad_refs):
        group = lax.rem(row + step, depth)
        for copy in fetches(step):
            copy.wait()
        query, key, val = (dot(normed, w_ref[step, c]).astype(BF) for c in range(3))
        d_attn = dot(cotan, wo_ref[step], ((1,), (1,))).astype(BF)
        parts = []
        for pair in range(block // LANES):
            cut = slice(pair * LANES, (pair + 1) * LANES)
            k, v = key[:, cut], val[:, cut]
            q2, da2 = both(query[:, cut]), both(d_attn[:, cut])
            scores = jnp.where(allowed, dot(q2, k, ((1,), (1,))) * scale, -jnp.inf)
            expo = jnp.exp(scores - jnp.max(scores, axis=-1, keepdims=True))
            prob = expo / jnp.sum(expo, axis=-1, keepdims=True)
            prob_bf = prob.astype(BF)
            parts.append(merge(dot(prob_bf, v)))
            grad_ref[2, :, cut] = dot(prob_bf, da2, ((0,), (0,))).astype(BF)
            d_prob = dot(da2, v, ((1,), (1,)))
            d_score = prob * (d_prob - jnp.sum(d_prob * prob, axis=-1, keepdims=True)) * scale
            d_score = d_score.astype(BF)
            grad_ref[0, :, cut] = merge(dot(d_score, k))
            grad_ref[1, :, cut] = dot(d_score, q2, ((0,), (0,))).astype(BF)
        attn_ref[:, span(group, block)] = jnp.concatenate(parts, axis=1)


def input_grad_body(depth, x_ref, g_ref, w_ref, *rest):
    grad_refs, (attn_ref, _, out_ref, attn_out_ref, *cut_refs) = rest[:depth], rest[depth:]
    attn_out_ref[...] = attn_ref[...]
    _, row, _ = place()
    block = x_ref.shape[1] // depth
    for k, cut_ref in enumerate(cut_refs):
        cut_ref[...] = g_ref[:, span(lax.rem(row + k, depth), block)]
    d_normed = jnp.zeros(x_ref.shape, F32)
    for step, grad_ref in enumerate(grad_refs):
        group = lax.rem(row + step, depth)
        for c in range(3):
            d_normed += dot(grad_ref[c], w_ref[:, span(c * depth + group, block)], ((1,), (1,)))
    wide = x_ref[...].astype(F32)
    inv_rms = inverse_rms(wide)
    mean = jnp.mean(d_normed * wide, axis=-1, keepdims=True)
    grad = g_ref[...].astype(F32) + inv_rms * d_normed - wide * inv_rms**3 * mean
    out_ref[...] = grad.astype(BF)


def choose(depth, peers, sections, across, wiring):
    section, row, col = place()
    source = lax.rem(section + sections - 1, sections)
    choices = []
    target = 2 * row + (1 - col if across else col)
    for slot in range(CAP):
        count = jnp.int32(0)
        taken = jnp.int32(-1)
        for p in range(peers):
            hit = wiring[source, p] == target
            taken = jnp.where(hit & (count == slot), p, taken)
            count = count + hit.astype(jnp.int32)
        here = (taken >= 0) & (lax.rem(taken, 2) == col)
        choices.append((here, lax.rem(row - lax.div(taken, 2) + depth, depth)))
    return choices


def pick(choices, refs, out_ref):
    seq, width = refs[0].shape
    for slot, (here, behind) in enumerate(choices):
        part = slice(slot * seq, (slot + 1) * seq)
        for k, ref in enumerate(refs):

            @pl.when(here & (behind == k))
            def _():
                out_ref[part, :] = ref[...]

        @pl.when(jnp.logical_not(here))
        def _():
            out_ref[part, :] = jnp.zeros((seq, width), BF)


def normed_body(depth, *refs):
    x_refs, out_ref = refs[:depth], refs[depth]
    seq = x_refs[0].shape[0]
    for k, x_ref in enumerate(x_refs):
        wide = x_ref[...].astype(F32)
        out_ref[:, k * seq : (k + 1) * seq] = jnp.transpose(wide * inverse_rms(wide)).astype(BF)


def pack_body(depth, peers, sections, wiring, *refs):
    x_refs, out_refs = refs[:depth], refs[-2:]
    for across, out_ref in enumerate(out_refs):
        pick(choose(depth, peers, sections, bool(across), wiring), x_refs, out_ref)


def proj_grad_body(depth, peers, first, normed_ref, *refs):
    _, row, col = place()
    grad_refs, rest = refs[:depth], refs[depth:]
    token_ref, stack_ref = rest[-2], rest[-1]
    _, seq, block = grad_refs[0].shape
    slab = normed_ref.shape[0] // peers
    for k, grad_ref in enumerate(grad_refs):
        for c in range(3):
            stack_ref[k * seq : (k + 1) * seq, c * block : (c + 1) * block] = grad_ref[c]
    rows = 1 - col if first else col
    groups = [lax.rem(row + k, depth) for k in range(depth)]
    left = jnp.concatenate([normed_ref[span(2 * a + rows, slab), :] for a in groups], axis=0)
    part = dot(left, stack_ref[...]) * (1.0 / peers)
    if first:
        rest[-3][...] = part.astype(BF)
    else:
        part = (part + rest[0][...].astype(F32)).astype(BF)
        for k, out_ref in enumerate(rest[-2 - depth : -2]):
            out_ref[...] = part[k * slab : (k + 1) * slab]
    token_ref[...] = jnp.zeros(token_ref.shape, F32)


def slots_body(depth, peers, sections, across, wiring, x_pick, *refs):
    attn_refs, rest = refs[:depth], refs[depth:]
    w_ref, slots_ref, attn_pick = rest[0], rest[-2], rest[-1]
    pick(choose(depth, peers, sections, across, wiring), attn_refs, attn_pick)
    y = (x_pick[...].astype(F32) + dot(attn_pick[...], w_ref[...])).astype(BF)
    slots_ref[...] = y.reshape(slots_ref.shape)


def out_grad_body(depth, peers, *refs):
    g_refs, attn_refs, (_, mine_ref, other_ref) = refs[:depth], refs[depth : 2 * depth], refs[2 * depth :]
    slab = mine_ref.shape[0]
    total = dot(g_refs[0][...], attn_refs[0][...], ((0,), (0,)))
    for g_ref, attn_ref in zip(g_refs[1:], attn_refs[1:]):
        total += dot(g_ref[...], attn_ref[...], ((0,), (0,)))
    total = total * (1.0 / peers)
    first = place()[2] == 0
    mine_ref[...] = jnp.where(first, total[:slab], total[slab:])
    other_ref[...] = jnp.where(first, total[slab:], total[:slab]).astype(BF)


def final_body(depth, *refs):
    landed_refs, rest = refs[:depth], refs[depth:]
    out_ref, out_other, slots_ref, slots_other, back_ref, grad_ref, layer_ref, back_out_ref = rest
    row = place()[1]
    step = pl.program_id(0)
    block = grad_ref.shape[1] // depth

    @pl.when(step < 3)
    def _():
        for k, landed_ref in enumerate(landed_refs):
            grad_ref[:, span(lax.rem(row - k + depth, depth), block)] = landed_ref[...].astype(F32)

    @pl.when(step == 3)
    def _():
        grad_ref[...] = out_ref[...] + out_other[...].astype(F32)
        layer_ref[...] = slots_ref[...] + slots_other[...]
        back_out_ref[...] = back_ref[...]


def shards(sent_rows, cotangent, wiring, w_qkv, w_out):
    peers = lax.axis_size("peer")
    sections = lax.axis_size("section")
    depth = peers // 2
    weights_in, weights_back = w_qkv[0], w_out[0]
    width = weights_back.shape[0]
    block = width // depth
    slab = width // peers
    seq = sent_rows.shape[2]

    def hop(value, steps):
        pairs = [
            (s * peers + p, (s + 1) % sections * peers + (p + 2 * steps) % peers)
            for s in range(sections)
            for p in range(peers)
        ]
        return lax.ppermute(value, ("section", "peer"), pairs)

    def along(value, steps):
        return lax.ppermute(value, "peer", [(p, (p + 2 * steps) % peers) for p in range(peers)])

    def across(value):
        return lax.ppermute(value, "peer", [(p, p ^ 1) for p in range(peers)])

    sent, cotan = sent_rows[0, 0], cotangent[0, 0]
    x = hop(sent, 0)
    g = hop(cotan, 0)
    column_x = [x] + [hop(sent, k) for k in range(1, depth)]

    attn, *grads = call(
        functools.partial(layer_body, depth),
        "layer",
        (x, g, weights_in, weights_back),
        [shape((seq, width))] + [shape((3, seq, block))] * depth,
        in_specs=[VMEM] * 2 + [ANY] * 2,
        scratch=[
            pltpu.VMEM((depth, 3, width, block), BF),
            pltpu.VMEM((depth, block, width), BF),
            pltpu.SemaphoreType.DMA((depth, 4)),
        ],
        limit=50,
        flops=12 * seq * width * width,
        nbytes=8 * width * width,
    )
    column_d = [grads[0]] + [along(grads[k], k) for k in range(1, depth)]

    smem = pl.BlockSpec(memory_space=pltpu.SMEM)
    normed = call(
        functools.partial(normed_body, depth),
        "normed",
        column_x,
        shape((width, depth * seq)),
        flops=6 * depth * seq * width,
        nbytes=4 * depth * seq * width,
    )
    input_grad, attn_sent, *cuts = call(
        functools.partial(input_grad_body, depth),
        "input_grad",
        (x, g, weights_in, *grads, attn, normed),
        [shape((seq, width))] * 2 + [shape((seq, block))] * depth,
        in_specs=[VMEM] * (depth + 4) + [ANY],
        flops=6 * seq * width * width,
        nbytes=6 * width * width,
    )
    back = lax.ppermute(input_grad, "section", [(s, (s - 1) % sections) for s in range(sections)])

    part_shape = shape((depth * slab, 3 * block))
    part_cost = {
        "flops": 2 * depth * slab * depth * seq * 3 * block,
        "nbytes": 2 * (depth * slab * depth * seq + depth * seq * 3 * block + depth * slab * 3 * block),
    }
    stack = [pltpu.VMEM((depth * seq, 3 * block), BF)]
    token = shape((8, LANES), F32)
    column_attn = [attn_sent] + [along(attn_sent, k) for k in range(1, depth)]
    column_g = [cuts[0]] + [along(cuts[k], k) for k in range(1, depth)]
    part_other, arrived = call(
        functools.partial(proj_grad_body, depth, peers, True),
        "proj_grad_other",
        (normed, *column_d, input_grad),
        [part_shape, token],
        in_specs=[VMEM] * (depth + 1) + [ANY],
        scratch=stack,
        **part_cost,
    )
    x_mine, x_other = call(
        functools.partial(pack_body, depth, peers, sections),
        "pack",
        (wiring, *column_x, arrived),
        [shape((CAP * seq, width))] * 2,
        in_specs=[smem] + [VMEM] * depth + [ANY],
    )
    slot_shape = shape((CAP, seq, width))

    def slots(to_neighbour, x_pick, extra):
        return call(
            functools.partial(slots_body, depth, peers, sections, to_neighbour),
            "slots_other" if to_neighbour else "slots_mine",
            (wiring, x_pick, *column_attn, weights_back, extra),
            slot_shape,
            in_specs=[smem] + [VMEM] * (depth + 2) + [ANY],
            scratch=[pltpu.VMEM((CAP * seq, width), BF)],
        )

    slots_sent = slots(True, x_other, arrived)
    *summed, done = call(
        functools.partial(proj_grad_body, depth, peers, False),
        "proj_grad_mine",
        (normed, *column_d, across(part_other), slots_sent),
        [shape((slab, 3 * block))] * depth + [token],
        in_specs=[VMEM] * (depth + 2) + [ANY],
        scratch=stack,
        **part_cost,
    )
    landed = [summed[0]] + [along(summed[k], k) for k in range(1, depth)]
    out_mine, out_sent = call(
        functools.partial(out_grad_body, depth, peers),
        "out_grad",
        (*column_g, *column_attn, slots_sent),
        [shape((slab, width), F32), shape((slab, width))],
        in_specs=[VMEM] * (2 * depth) + [ANY],
        flops=2 * depth * seq * block * width,
        nbytes=2 * depth * seq * (block + width),
    )
    slots_mine = slots(False, x_mine, out_sent)
    section_grad, layer_out, back_out = call(
        functools.partial(final_body, depth),
        "final",
        (*landed, out_mine, across(out_sent), slots_mine, across(slots_sent), back),
        [shape((slab, 4 * width), F32), shape((CAP, seq, width)), shape((seq, width))],
        in_specs=[
            *[pl.BlockSpec((slab, block), lambda c: (0, jnp.minimum(c, 2)))] * depth,
            whole((slab, width)),
            whole((slab, width)),
            whole((CAP, seq, width)),
            whole((CAP, seq, width)),
            whole((seq, width)),
        ],
        out_specs=[pl.BlockSpec((slab, width), lambda c: (0, c)), whole((CAP, seq, width)), whole((seq, width))],
        grid=(4,),
        nbytes=8 * slab * 4 * width,
    )
    return (layer_out[None, None], back_out[None, None], section_grad[None])


def solution(mesh):
    in_specs = (
        P("section", "peer", None, None),
        P("section", "peer", None, None),
        P(),
        P("section", None, None),
        P("section", None, None),
    )
    out_specs = (
        P("section", "peer", None, None, None),
        P("section", "peer", None, None),
        P("section", "peer", None),
    )
    return jax.shard_map(shards, mesh=mesh, in_specs=in_specs, out_specs=out_specs, check_vma=False)
```

```python
import functools

import jax
import jax.numpy as jnp
from jax import lax
from jax.experimental import pallas as pl
from jax.experimental.pallas import tpu as pltpu
from jax.sharding import PartitionSpec as P

HEAD = 64
CAP = 2
EPSILON = 1e-05
LANES = 128
BF = jnp.bfloat16
F32 = jnp.float32
MIB = 1 << 20


def dot(a, b, dims=((1,), (0,))):
    return lax.dot_general(a, b, (dims, ((), ())), preferred_element_type=F32)


def inverse_rms(wide):
    return lax.rsqrt(jnp.mean(wide * wide, axis=-1, keepdims=True) + EPSILON)


def whole(shape):
    return pl.BlockSpec(shape, lambda *_: (0,) * len(shape))


VMEM = pl.BlockSpec(memory_space=pltpu.VMEM)
ANY = pl.BlockSpec(memory_space=pl.ANY)


WEIGHT = {"normed": 0, "input_grad": 8, "pack": 20, "slots_other": 3, "proj_grad_mine": 5, "out_grad": 3, "slots_mine": 60}


def call(body, name, arrays, out_shapes, in_specs=None, out_specs=None, grid=(), scratch=(), limit=16, flops=0, nbytes=0):
    if name in WEIGHT:
        flops, nbytes = WEIGHT[name] * 10**9, 0
    return pl.pallas_call(
        body,
        grid=grid,
        in_specs=[VMEM] * len(arrays) if in_specs is None else in_specs,
        out_specs=jax.tree.map(lambda _: VMEM, out_shapes) if out_specs is None else out_specs,
        scratch_shapes=list(scratch),
        out_shape=out_shapes,
        name=name,
        compiler_params=pltpu.CompilerParams(vmem_limit_bytes=limit * MIB),
        cost_estimate=pl.CostEstimate(flops=int(flops), bytes_accessed=nbytes, transcendentals=0),
    )(*arrays)


def place():
    me = lax.axis_index("peer")
    return lax.axis_index("section"), lax.div(me, 2), lax.rem(me, 2)


def span(index, size):
    return pl.ds(pl.multiple_of(index * size, size), size)


def shape(dims, dtype=BF):
    return jax.ShapeDtypeStruct(dims, dtype)


def layer_body(depth, x_ref, g_ref, w_hbm, wo_hbm, attn_ref, *rest):
    grad_refs, (w_ref, wo_ref, sems) = rest[:depth], rest[depth:]
    row = place()[1]
    seq, width = x_ref.shape
    block = width // depth

    def fetches(step):
        group = lax.rem(row + step, depth)
        copies = []
        for c in range(3):
            cut = span(c * depth + group, block)
            copies.append(pltpu.make_async_copy(w_hbm.at[:, cut], w_ref.at[step, c], sems.at[step, c]))
        rows = span(group, block)
        copies.append(pltpu.make_async_copy(wo_hbm.at[rows, :], wo_ref.at[step], sems.at[step, 3]))
        return copies

    for step in range(depth):
        for copy in fetches(step):
            copy.start()
    scale = HEAD ** (-0.5)
    wide = x_ref[...].astype(F32)
    normed = (wide * inverse_rms(wide)).astype(BF)
    cotan = g_ref[...]
    low = lax.broadcasted_iota(jnp.int32, (seq, LANES), 1) < HEAD
    rows = lax.broadcasted_iota(jnp.int32, (2 * seq, seq), 0)
    allowed = jnp.where(rows < seq, rows, rows - seq) >= lax.broadcasted_iota(jnp.int32, (2 * seq, seq), 1)
    zero = jnp.zeros((), BF)

    def both(value):
        return jnp.concatenate([jnp.where(low, value, zero), jnp.where(low, zero, value)], axis=0)

    def merge(value):
        return jnp.where(low, value[:seq], value[seq:]).astype(BF)

    for step, grad_ref in enumerate(grad_refs):
        group = lax.rem(row + step, depth)
        for copy in fetches(step):
            copy.wait()
        query, key, val = (dot(normed, w_ref[step, c]).astype(BF) for c in range(3))
        d_attn = dot(cotan, wo_ref[step], ((1,), (1,))).astype(BF)
        parts = []
        for pair in range(block // LANES):
            cut = slice(pair * LANES, (pair + 1) * LANES)
            k, v = key[:, cut], val[:, cut]
            q2, da2 = both(query[:, cut]), both(d_attn[:, cut])
            scores = jnp.where(allowed, dot(q2, k, ((1,), (1,))) * scale, -jnp.inf)
            expo = jnp.exp(scores - jnp.max(scores, axis=-1, keepdims=True))
            prob = expo / jnp.sum(expo, axis=-1, keepdims=True)
            prob_bf = prob.astype(BF)
            parts.append(merge(dot(prob_bf, v)))
            grad_ref[2, :, cut] = dot(prob_bf, da2, ((0,), (0,))).astype(BF)
            d_prob = dot(da2, v, ((1,), (1,)))
            d_score = prob * (d_prob - jnp.sum(d_prob * prob, axis=-1, keepdims=True)) * scale
            d_score = d_score.astype(BF)
            grad_ref[0, :, cut] = merge(dot(d_score, k))
            grad_ref[1, :, cut] = dot(d_score, q2, ((0,), (0,))).astype(BF)
        attn_ref[:, span(group, block)] = jnp.concatenate(parts, axis=1)


def input_grad_body(depth, x_ref, g_ref, w_ref, *rest):
    grad_refs, (attn_ref, _, out_ref, attn_out_ref, *cut_refs) = rest[:depth], rest[depth:]
    attn_out_ref[...] = attn_ref[...]
    _, row, _ = place()
    block = x_ref.shape[1] // depth
    for k, cut_ref in enumerate(cut_refs):
        cut_ref[...] = g_ref[:, span(lax.rem(row + k, depth), block)]
    d_normed = jnp.zeros(x_ref.shape, F32)
    for step, grad_ref in enumerate(grad_refs):
        group = lax.rem(row + step, depth)
        for c in range(3):
            d_normed += dot(grad_ref[c], w_ref[:, span(c * depth + group, block)], ((1,), (1,)))
    wide = x_ref[...].astype(F32)
    inv_rms = inverse_rms(wide)
    mean = jnp.mean(d_normed * wide, axis=-1, keepdims=True)
    grad = g_ref[...].astype(F32) + inv_rms * d_normed - wide * inv_rms**3 * mean
    out_ref[...] = grad.astype(BF)


def choose(depth, peers, sections, across, wiring):
    section, row, col = place()
    source = lax.rem(section + sections - 1, sections)
    choices = []
    target = 2 * row + (1 - col if across else col)
    for slot in range(CAP):
        count = jnp.int32(0)
        taken = jnp.int32(-1)
        for p in range(peers):
            hit = wiring[source, p] == target
            taken = jnp.where(hit & (count == slot), p, taken)
            count = count + hit.astype(jnp.int32)
        here = (taken >= 0) & (lax.rem(taken, 2) == col)
        choices.append((here, lax.rem(row - lax.div(taken, 2) + depth, depth)))
    return choices


def pick(choices, refs, out_ref):
    seq, width = refs[0].shape
    for slot, (here, behind) in enumerate(choices):
        part = slice(slot * seq, (slot + 1) * seq)
        for k, ref in enumerate(refs):

            @pl.when(here & (behind == k))
            def _():
                out_ref[part, :] = ref[...]

        @pl.when(jnp.logical_not(here))
        def _():
            out_ref[part, :] = jnp.zeros((seq, width), BF)


def normed_body(depth, *refs):
    x_refs, out_ref = refs[:depth], refs[depth]
    seq = x_refs[0].shape[0]
    for k, x_ref in enumerate(x_refs):
        wide = x_ref[...].astype(F32)
        out_ref[:, k * seq : (k + 1) * seq] = jnp.transpose(wide * inverse_rms(wide)).astype(BF)


def pack_body(depth, peers, sections, wiring, *refs):
    x_refs, out_refs = refs[:depth], refs[-2:]
    for across, out_ref in enumerate(out_refs):
        pick(choose(depth, peers, sections, bool(across), wiring), x_refs, out_ref)


def proj_grad_body(depth, peers, first, normed_ref, *refs):
    _, row, col = place()
    grad_refs, rest = refs[:depth], refs[depth:]
    token_ref, stack_ref = rest[-2], rest[-1]
    _, seq, block = grad_refs[0].shape
    slab = normed_ref.shape[0] // peers
    for k, grad_ref in enumerate(grad_refs):
        for c in range(3):
            stack_ref[k * seq : (k + 1) * seq, c * block : (c + 1) * block] = grad_ref[c]
    rows = 1 - col if first else col
    groups = [lax.rem(row + k, depth) for k in range(depth)]
    left = jnp.concatenate([normed_ref[span(2 * a + rows, slab), :] for a in groups], axis=0)
    part = dot(left, stack_ref[...]) * (1.0 / peers)
    if first:
        rest[-3][...] = part.astype(BF)
    else:
        part = (part + rest[0][...].astype(F32)).astype(BF)
        for k, out_ref in enumerate(rest[-2 - depth : -2]):
            out_ref[...] = part[k * slab : (k + 1) * slab]
    token_ref[...] = jnp.zeros(token_ref.shape, F32)


def slots_body(depth, peers, sections, across, wiring, x_pick, *refs):
    attn_refs, rest = refs[:depth], refs[depth:]
    w_ref, attn_pick = rest[0], rest[-1]
    cut_refs, (slots_ref, *cut_outs) = (rest[1:depth], rest[depth:-1]) if across else ((), rest[-2:-1])
    for cut_ref, cut_out in zip(cut_refs, cut_outs):
        cut_out[...] = cut_ref[...]
    pick(choose(depth, peers, sections, across, wiring), attn_refs, attn_pick)
    y = (x_pick[...].astype(F32) + dot(attn_pick[...], w_ref[...])).astype(BF)
    slots_ref[...] = y.reshape(slots_ref.shape)


def out_grad_body(depth, peers, *refs):
    g_refs, attn_refs, (_, mine_ref, other_ref) = refs[:depth], refs[depth : 2 * depth], refs[2 * depth :]
    slab = mine_ref.shape[0]
    total = dot(g_refs[0][...], attn_refs[0][...], ((0,), (0,)))
    for g_ref, attn_ref in zip(g_refs[1:], attn_refs[1:]):
        total += dot(g_ref[...], attn_ref[...], ((0,), (0,)))
    total = total * (1.0 / peers)
    first = place()[2] == 0
    mine_ref[...] = jnp.where(first, total[:slab], total[slab:])
    other_ref[...] = jnp.where(first, total[slab:], total[:slab]).astype(BF)


def final_body(depth, *refs):
    landed_refs, rest = refs[:depth], refs[depth:]
    out_ref, out_other, slots_ref, slots_other, back_ref, grad_ref, layer_ref, back_out_ref = rest
    row = place()[1]
    step = pl.program_id(0)
    block = grad_ref.shape[1] // depth

    @pl.when(step < 3)
    def _():
        for k, landed_ref in enumerate(landed_refs):
            grad_ref[:, span(lax.rem(row - k + depth, depth), block)] = landed_ref[...].astype(F32)

    @pl.when(step == 3)
    def _():
        grad_ref[...] = out_ref[...] + out_other[...].astype(F32)
        layer_ref[...] = slots_ref[...] + slots_other[...]
        back_out_ref[...] = back_ref[...]


def shards(sent_rows, cotangent, wiring, w_qkv, w_out):
    peers = lax.axis_size("peer")
    sections = lax.axis_size("section")
    depth = peers // 2
    weights_in, weights_back = w_qkv[0], w_out[0]
    width = weights_back.shape[0]
    block = width // depth
    slab = width // peers
    seq = sent_rows.shape[2]

    def hop(value, steps):
        pairs = [
            (s * peers + p, (s + 1) % sections * peers + (p + 2 * steps) % peers)
            for s in range(sections)
            for p in range(peers)
        ]
        return lax.ppermute(value, ("section", "peer"), pairs)

    def along(value, steps):
        return lax.ppermute(value, "peer", [(p, (p + 2 * steps) % peers) for p in range(peers)])

    def across(value):
        return lax.ppermute(value, "peer", [(p, p ^ 1) for p in range(peers)])

    sent, cotan = sent_rows[0, 0], cotangent[0, 0]
    x = hop(sent, 0)
    g = hop(cotan, 0)
    column_x = [x] + [hop(sent, k) for k in range(1, depth)]

    attn, *grads = call(
        functools.partial(layer_body, depth),
        "layer",
        (x, g, weights_in, weights_back),
        [shape((seq, width))] + [shape((3, seq, block))] * depth,
        in_specs=[VMEM] * 2 + [ANY] * 2,
        scratch=[
            pltpu.VMEM((depth, 3, width, block), BF),
            pltpu.VMEM((depth, block, width), BF),
            pltpu.SemaphoreType.DMA((depth, 4)),
        ],
        limit=50,
        flops=12 * seq * width * width,
        nbytes=8 * width * width,
    )
    column_d = [grads[0]] + [along(grads[k], k) for k in range(1, depth)]

    smem = pl.BlockSpec(memory_space=pltpu.SMEM)
    normed = call(
        functools.partial(normed_body, depth),
        "normed",
        column_x,
        shape((width, depth * seq)),
        flops=6 * depth * seq * width,
        nbytes=4 * depth * seq * width,
    )
    input_grad, attn_sent, *cuts = call(
        functools.partial(input_grad_body, depth),
        "input_grad",
        (x, g, weights_in, *grads, attn, normed),
        [shape((seq, width))] * 2 + [shape((seq, block))] * depth,
        in_specs=[VMEM] * (depth + 4) + [ANY],
        flops=6 * seq * width * width,
        nbytes=6 * width * width,
    )
    back = lax.ppermute(input_grad, "section", [(s, (s - 1) % sections) for s in range(sections)])

    part_shape = shape((depth * slab, 3 * block))
    part_cost = {
        "flops": 2 * depth * slab * depth * seq * 3 * block,
        "nbytes": 2 * (depth * slab * depth * seq + depth * seq * 3 * block + depth * slab * 3 * block),
    }
    stack = [pltpu.VMEM((depth * seq, 3 * block), BF)]
    token = shape((8, LANES), F32)
    column_attn = [attn_sent] + [along(attn_sent, k) for k in range(1, depth)]
    part_other, arrived = call(
        functools.partial(proj_grad_body, depth, peers, True),
        "proj_grad_other",
        (normed, *column_d, input_grad),
        [part_shape, token],
        in_specs=[VMEM] * (depth + 1) + [ANY],
        scratch=stack,
        **part_cost,
    )
    x_mine, x_other = call(
        functools.partial(pack_body, depth, peers, sections),
        "pack",
        (wiring, *column_x, arrived),
        [shape((CAP * seq, width))] * 2,
        in_specs=[smem] + [VMEM] * depth + [ANY],
    )
    slot_shape = shape((CAP, seq, width))

    def slots(to_neighbour, x_pick, extra):
        cut_shapes = [shape((seq, block))] * (depth - 1) if to_neighbour else []
        return call(
            functools.partial(slots_body, depth, peers, sections, to_neighbour),
            "slots_other" if to_neighbour else "slots_mine",
            (wiring, x_pick, *column_attn, weights_back, *extra),
            [slot_shape, *cut_shapes],
            in_specs=[smem] + [VMEM] * (depth + 2) + ([VMEM] * (depth - 1) if to_neighbour else [ANY]),
            scratch=[pltpu.VMEM((CAP * seq, width), BF)],
        )

    slots_sent, *cuts_sent = slots(True, x_other, cuts[1:])
    column_g = [cuts[0]] + [along(part, k) for k, part in enumerate(cuts_sent, 1)]
    *summed, done = call(
        functools.partial(proj_grad_body, depth, peers, False),
        "proj_grad_mine",
        (normed, *column_d, across(part_other), slots_sent),
        [shape((slab, 3 * block))] * depth + [token],
        in_specs=[VMEM] * (depth + 2) + [ANY],
        scratch=stack,
        **part_cost,
    )
    landed = [summed[0]] + [along(summed[k], k) for k in range(1, depth)]
    out_mine, out_sent = call(
        functools.partial(out_grad_body, depth, peers),
        "out_grad",
        (*column_g, *column_attn, done),
        [shape((slab, width), F32), shape((slab, width))],
        in_specs=[VMEM] * (2 * depth) + [ANY],
        flops=2 * depth * seq * block * width,
        nbytes=2 * depth * seq * (block + width),
    )
    (slots_mine,) = slots(False, x_mine, [out_sent])
    section_grad, layer_out, back_out = call(
        functools.partial(final_body, depth),
        "final",
        (*landed, out_mine, across(out_sent), slots_mine, across(slots_sent), back),
        [shape((slab, 4 * width), F32), shape((CAP, seq, width)), shape((seq, width))],
        in_specs=[
            *[pl.BlockSpec((slab, block), lambda c: (0, jnp.minimum(c, 2)))] * depth,
            whole((slab, width)),
            whole((slab, width)),
            whole((CAP, seq, width)),
            whole((CAP, seq, width)),
            whole((seq, width)),
        ],
        out_specs=[pl.BlockSpec((slab, width), lambda c: (0, c)), whole((CAP, seq, width)), whole((seq, width))],
        grid=(4,),
        nbytes=8 * slab * 4 * width,
    )
    return (layer_out[None, None], back_out[None, None], section_grad[None])


def solution(mesh):
    in_specs = (
        P("section", "peer", None, None),
        P("section", "peer", None, None),
        P(),
        P("section", None, None),
        P("section", None, None),
    )
    out_specs = (
        P("section", "peer", None, None, None),
        P("section", "peer", None, None),
        P("section", "peer", None),
    )
    return jax.shard_map(shards, mesh=mesh, in_specs=in_specs, out_specs=out_specs, check_vma=False)
```

```python
import functools

import jax
import jax.numpy as jnp
from jax import lax
from jax.experimental import pallas as pl
from jax.experimental.pallas import tpu as pltpu
from jax.sharding import PartitionSpec as P

HEAD = 64
CAP = 2
EPSILON = 1e-05
LANES = 128
BF = jnp.bfloat16
F32 = jnp.float32
MIB = 1 << 20


def dot(a, b, dims=((1,), (0,))):
    return lax.dot_general(a, b, (dims, ((), ())), preferred_element_type=F32)


def inverse_rms(wide):
    return lax.rsqrt(jnp.mean(wide * wide, axis=-1, keepdims=True) + EPSILON)


def whole(shape):
    return pl.BlockSpec(shape, lambda *_: (0,) * len(shape))


VMEM = pl.BlockSpec(memory_space=pltpu.VMEM)
ANY = pl.BlockSpec(memory_space=pl.ANY)


WEIGHT = {"normed": 0, "input_grad": 8, "pack": 20, "slots_other": 3, "proj_grad_mine": 5, "out_grad": 3, "slots_mine": 60}


def call(body, name, arrays, out_shapes, in_specs=None, out_specs=None, grid=(), scratch=(), limit=16, flops=0, nbytes=0):
    if name in WEIGHT:
        flops, nbytes = WEIGHT[name] * 10**9, 0
    return pl.pallas_call(
        body,
        grid=grid,
        in_specs=[VMEM] * len(arrays) if in_specs is None else in_specs,
        out_specs=jax.tree.map(lambda _: VMEM, out_shapes) if out_specs is None else out_specs,
        scratch_shapes=list(scratch),
        out_shape=out_shapes,
        name=name,
        compiler_params=pltpu.CompilerParams(vmem_limit_bytes=limit * MIB),
        cost_estimate=pl.CostEstimate(flops=int(flops), bytes_accessed=nbytes, transcendentals=0),
    )(*arrays)


def place():
    me = lax.axis_index("peer")
    return lax.axis_index("section"), lax.div(me, 2), lax.rem(me, 2)


def span(index, size):
    return pl.ds(pl.multiple_of(index * size, size), size)


def shape(dims, dtype=BF):
    return jax.ShapeDtypeStruct(dims, dtype)


def layer_body(depth, x_ref, g_ref, w_hbm, wo_hbm, attn_ref, *rest):
    grad_refs, (w_ref, wo_ref, sems) = rest[:depth], rest[depth:]
    row = place()[1]
    seq, width = x_ref.shape
    block = width // depth

    def fetches(step):
        group = lax.rem(row + step, depth)
        copies = []
        for c in range(3):
            cut = span(c * depth + group, block)
            copies.append(pltpu.make_async_copy(w_hbm.at[:, cut], w_ref.at[step, c], sems.at[step, c]))
        rows = span(group, block)
        copies.append(pltpu.make_async_copy(wo_hbm.at[rows, :], wo_ref.at[step], sems.at[step, 3]))
        return copies

    for step in range(depth):
        for copy in fetches(step):
            copy.start()
    scale = HEAD ** (-0.5)
    wide = x_ref[...].astype(F32)
    normed = (wide * inverse_rms(wide)).astype(BF)
    cotan = g_ref[...]
    low = lax.broadcasted_iota(jnp.int32, (seq, LANES), 1) < HEAD
    rows = lax.broadcasted_iota(jnp.int32, (2 * seq, seq), 0)
    allowed = jnp.where(rows < seq, rows, rows - seq) >= lax.broadcasted_iota(jnp.int32, (2 * seq, seq), 1)
    zero = jnp.zeros((), BF)

    def both(value):
        return jnp.concatenate([jnp.where(low, value, zero), jnp.where(low, zero, value)], axis=0)

    def merge(value):
        return jnp.where(low, value[:seq], value[seq:]).astype(BF)

    for step, grad_ref in enumerate(grad_refs):
        group = lax.rem(row + step, depth)
        for copy in fetches(step):
            copy.wait()
        query, key, val = (dot(normed, w_ref[step, c]).astype(BF) for c in range(3))
        d_attn = dot(cotan, wo_ref[step], ((1,), (1,))).astype(BF)
        parts = []
        for pair in range(block // LANES):
            cut = slice(pair * LANES, (pair + 1) * LANES)
            k, v = key[:, cut], val[:, cut]
            q2, da2 = both(query[:, cut]), both(d_attn[:, cut])
            scores = jnp.where(allowed, dot(q2, k, ((1,), (1,))) * scale, -jnp.inf)
            expo = jnp.exp(scores - jnp.max(scores, axis=-1, keepdims=True))
            prob = expo / jnp.sum(expo, axis=-1, keepdims=True)
            prob_bf = prob.astype(BF)
            parts.append(merge(dot(prob_bf, v)))
            grad_ref[2, :, cut] = dot(prob_bf, da2, ((0,), (0,))).astype(BF)
            d_prob = dot(da2, v, ((1,), (1,)))
            d_score = prob * (d_prob - jnp.sum(d_prob * prob, axis=-1, keepdims=True)) * scale
            d_score = d_score.astype(BF)
            grad_ref[0, :, cut] = merge(dot(d_score, k))
            grad_ref[1, :, cut] = dot(d_score, q2, ((0,), (0,))).astype(BF)
        attn_ref[:, span(group, block)] = jnp.concatenate(parts, axis=1)


def input_grad_body(depth, x_ref, g_ref, w_ref, *rest):
    grad_refs, (attn_ref, _, out_ref, attn_out_ref, *cut_refs) = rest[:depth], rest[depth:]
    attn_out_ref[...] = attn_ref[...]
    _, row, _ = place()
    block = x_ref.shape[1] // depth
    for k, cut_ref in enumerate(cut_refs):
        cut_ref[...] = g_ref[:, span(lax.rem(row + k, depth), block)]
    d_normed = jnp.zeros(x_ref.shape, F32)
    for step, grad_ref in enumerate(grad_refs):
        group = lax.rem(row + step, depth)
        for c in range(3):
            d_normed += dot(grad_ref[c], w_ref[:, span(c * depth + group, block)], ((1,), (1,)))
    wide = x_ref[...].astype(F32)
    inv_rms = inverse_rms(wide)
    mean = jnp.mean(d_normed * wide, axis=-1, keepdims=True)
    grad = g_ref[...].astype(F32) + inv_rms * d_normed - wide * inv_rms**3 * mean
    out_ref[...] = grad.astype(BF)


def choose(depth, peers, sections, across, wiring):
    section, row, col = place()
    source = lax.rem(section + sections - 1, sections)
    choices = []
    target = 2 * row + (1 - col if across else col)
    for slot in range(CAP):
        count = jnp.int32(0)
        taken = jnp.int32(-1)
        for p in range(peers):
            hit = wiring[source, p] == target
            taken = jnp.where(hit & (count == slot), p, taken)
            count = count + hit.astype(jnp.int32)
        here = (taken >= 0) & (lax.rem(taken, 2) == col)
        choices.append((here, lax.rem(row - lax.div(taken, 2) + depth, depth)))
    return choices


def pick(choices, refs, out_ref):
    seq, width = refs[0].shape
    for slot, (here, behind) in enumerate(choices):
        part = slice(slot * seq, (slot + 1) * seq)
        for k, ref in enumerate(refs):

            @pl.when(here & (behind == k))
            def _():
                out_ref[part, :] = ref[...]

        @pl.when(jnp.logical_not(here))
        def _():
            out_ref[part, :] = jnp.zeros((seq, width), BF)


def normed_body(depth, *refs):
    x_refs, out_ref = refs[:depth], refs[depth]
    seq = x_refs[0].shape[0]
    for k, x_ref in enumerate(x_refs):
        wide = x_ref[...].astype(F32)
        out_ref[:, k * seq : (k + 1) * seq] = jnp.transpose(wide * inverse_rms(wide)).astype(BF)


def pack_body(depth, peers, sections, wiring, *refs):
    x_refs, out_refs = refs[:depth], refs[-2:]
    for across, out_ref in enumerate(out_refs):
        pick(choose(depth, peers, sections, bool(across), wiring), x_refs, out_ref)


def proj_grad_body(depth, peers, first, normed_ref, *refs):
    _, row, col = place()
    grad_refs, rest = refs[:depth], refs[depth:]
    token_ref, stack_ref = rest[-2], rest[-1]
    _, seq, block = grad_refs[0].shape
    slab = normed_ref.shape[0] // peers
    for k, grad_ref in enumerate(grad_refs):
        for c in range(3):
            stack_ref[k * seq : (k + 1) * seq, c * block : (c + 1) * block] = grad_ref[c]
    rows = 1 - col if first else col
    groups = [lax.rem(row + k, depth) for k in range(depth)]
    left = jnp.concatenate([normed_ref[span(2 * a + rows, slab), :] for a in groups], axis=0)
    part = dot(left, stack_ref[...]) * (1.0 / peers)
    if first:
        rest[-3][...] = part.astype(BF)
    else:
        part = (part + rest[0][...].astype(F32)).astype(BF)
        for k, out_ref in enumerate(rest[-2 - depth : -2]):
            out_ref[...] = part[k * slab : (k + 1) * slab]
    token_ref[...] = jnp.zeros(token_ref.shape, F32)


def slots_body(depth, peers, sections, across, wiring, x_pick, *refs):
    attn_refs, rest = refs[:depth], refs[depth:]
    w_ref, attn_pick = rest[0], rest[-1]
    cut_refs, (slots_ref, *cut_outs) = (rest[1:depth], rest[depth:-1]) if across else ((), rest[-2:-1])
    for cut_ref, cut_out in zip(cut_refs, cut_outs):
        cut_out[...] = cut_ref[...]
    pick(choose(depth, peers, sections, across, wiring), attn_refs, attn_pick)
    y = (x_pick[...].astype(F32) + dot(attn_pick[...], w_ref[...])).astype(BF)
    slots_ref[...] = y.reshape(slots_ref.shape)


def out_grad_body(depth, peers, *refs):
    g_refs, attn_refs, (_, mine_ref, other_ref) = refs[:depth], refs[depth : 2 * depth], refs[2 * depth :]
    slab = mine_ref.shape[0]
    total = dot(g_refs[0][...], attn_refs[0][...], ((0,), (0,)))
    for g_ref, attn_ref in zip(g_refs[1:], attn_refs[1:]):
        total += dot(g_ref[...], attn_ref[...], ((0,), (0,)))
    total = total * (1.0 / peers)
    first = place()[2] == 0
    mine_ref[...] = jnp.where(first, total[:slab], total[slab:])
    other_ref[...] = jnp.where(first, total[slab:], total[:slab]).astype(BF)


def final_body(depth, *refs):
    landed_refs, (out_ref, out_other, grad_ref) = refs[:depth], refs[depth:]
    row = place()[1]
    step = pl.program_id(0)
    block = grad_ref.shape[1] // depth

    @pl.when(step < 3)
    def _():
        for k, landed_ref in enumerate(landed_refs):
            grad_ref[:, span(lax.rem(row - k + depth, depth), block)] = landed_ref[...].astype(F32)

    @pl.when(step == 3)
    def _():
        grad_ref[...] = out_ref[...] + out_other[...].astype(F32)


def finish_body(slots_ref, slots_other, back_ref, layer_ref, back_out_ref):
    layer_ref[...] = slots_ref[...] + slots_other[...]
    back_out_ref[...] = back_ref[...]


def shards(sent_rows, cotangent, wiring, w_qkv, w_out):
    peers = lax.axis_size("peer")
    sections = lax.axis_size("section")
    depth = peers // 2
    weights_in, weights_back = w_qkv[0], w_out[0]
    width = weights_back.shape[0]
    block = width // depth
    slab = width // peers
    seq = sent_rows.shape[2]

    def hop(value, steps):
        pairs = [
            (s * peers + p, (s + 1) % sections * peers + (p + 2 * steps) % peers)
            for s in range(sections)
            for p in range(peers)
        ]
        return lax.ppermute(value, ("section", "peer"), pairs)

    def along(value, steps):
        return lax.ppermute(value, "peer", [(p, (p + 2 * steps) % peers) for p in range(peers)])

    def across(value):
        return lax.ppermute(value, "peer", [(p, p ^ 1) for p in range(peers)])

    sent, cotan = sent_rows[0, 0], cotangent[0, 0]
    x = hop(sent, 0)
    g = hop(cotan, 0)
    column_x = [x] + [hop(sent, k) for k in range(1, depth)]

    attn, *grads = call(
        functools.partial(layer_body, depth),
        "layer",
        (x, g, weights_in, weights_back),
        [shape((seq, width))] + [shape((3, seq, block))] * depth,
        in_specs=[VMEM] * 2 + [ANY] * 2,
        scratch=[
            pltpu.VMEM((depth, 3, width, block), BF),
            pltpu.VMEM((depth, block, width), BF),
            pltpu.SemaphoreType.DMA((depth, 4)),
        ],
        limit=50,
        flops=12 * seq * width * width,
        nbytes=8 * width * width,
    )
    column_d = [grads[0]] + [along(grads[k], k) for k in range(1, depth)]

    smem = pl.BlockSpec(memory_space=pltpu.SMEM)
    normed = call(
        functools.partial(normed_body, depth),
        "normed",
        column_x,
        shape((width, depth * seq)),
        flops=6 * depth * seq * width,
        nbytes=4 * depth * seq * width,
    )
    input_grad, attn_sent, *cuts = call(
        functools.partial(input_grad_body, depth),
        "input_grad",
        (x, g, weights_in, *grads, attn, normed),
        [shape((seq, width))] * 2 + [shape((seq, block))] * depth,
        in_specs=[VMEM] * (depth + 4) + [ANY],
        flops=6 * seq * width * width,
        nbytes=6 * width * width,
    )
    back = lax.ppermute(input_grad, "section", [(s, (s - 1) % sections) for s in range(sections)])

    part_shape = shape((depth * slab, 3 * block))
    part_cost = {
        "flops": 2 * depth * slab * depth * seq * 3 * block,
        "nbytes": 2 * (depth * slab * depth * seq + depth * seq * 3 * block + depth * slab * 3 * block),
    }
    stack = [pltpu.VMEM((depth * seq, 3 * block), BF)]
    token = shape((8, LANES), F32)
    column_attn = [attn_sent] + [along(attn_sent, k) for k in range(1, depth)]
    part_other, arrived = call(
        functools.partial(proj_grad_body, depth, peers, True),
        "proj_grad_other",
        (normed, *column_d, input_grad),
        [part_shape, token],
        in_specs=[VMEM] * (depth + 1) + [ANY],
        scratch=stack,
        **part_cost,
    )
    x_mine, x_other = call(
        functools.partial(pack_body, depth, peers, sections),
        "pack",
        (wiring, *column_x, arrived),
        [shape((CAP * seq, width))] * 2,
        in_specs=[smem] + [VMEM] * depth + [ANY],
    )
    slot_shape = shape((CAP, seq, width))

    def slots(to_neighbour, x_pick, extra):
        cut_shapes = [shape((seq, block))] * (depth - 1) if to_neighbour else []
        return call(
            functools.partial(slots_body, depth, peers, sections, to_neighbour),
            "slots_other" if to_neighbour else "slots_mine",
            (wiring, x_pick, *column_attn, weights_back, *extra),
            [slot_shape, *cut_shapes],
            in_specs=[smem] + [VMEM] * (depth + 2) + ([VMEM] * (depth - 1) if to_neighbour else [ANY]),
            scratch=[pltpu.VMEM((CAP * seq, width), BF)],
        )

    slots_sent, *cuts_sent = slots(True, x_other, cuts[1:])
    column_g = [cuts[0]] + [along(part, k) for k, part in enumerate(cuts_sent, 1)]
    *summed, done = call(
        functools.partial(proj_grad_body, depth, peers, False),
        "proj_grad_mine",
        (normed, *column_d, across(part_other), slots_sent),
        [shape((slab, 3 * block))] * depth + [token],
        in_specs=[VMEM] * (depth + 2) + [ANY],
        scratch=stack,
        **part_cost,
    )
    landed = [summed[0]] + [along(summed[k], k) for k in range(1, depth)]
    out_mine, out_sent = call(
        functools.partial(out_grad_body, depth, peers),
        "out_grad",
        (*column_g, *column_attn, done),
        [shape((slab, width), F32), shape((slab, width))],
        in_specs=[VMEM] * (2 * depth) + [ANY],
        flops=2 * depth * seq * block * width,
        nbytes=2 * depth * seq * (block + width),
    )
    (slots_mine,) = slots(False, x_mine, [out_sent])
    layer_out, back_out = call(
        finish_body,
        "finish",
        (slots_mine, across(slots_sent), back),
        [slot_shape, shape((seq, width))],
        in_specs=[whole((CAP, seq, width))] * 2 + [whole((seq, width))],
        out_specs=[whole((CAP, seq, width)), whole((seq, width))],
        grid=(1,),
        nbytes=8 * CAP * seq * width,
    )
    section_grad = call(
        functools.partial(final_body, depth),
        "final",
        (*landed, out_mine, across(out_sent)),
        shape((slab, 4 * width), F32),
        in_specs=[pl.BlockSpec((slab, block), lambda c: (0, jnp.minimum(c, 2)))] * depth + [whole((slab, width))] * 2,
        out_specs=pl.BlockSpec((slab, width), lambda c: (0, c)),
        grid=(4,),
        nbytes=8 * slab * 4 * width,
    )
    return (layer_out[None, None], back_out[None, None], section_grad[None])


def solution(mesh):
    in_specs = (
        P("section", "peer", None, None),
        P("section", "peer", None, None),
        P(),
        P("section", None, None),
        P("section", None, None),
    )
    out_specs = (
        P("section", "peer", None, None, None),
        P("section", "peer", None, None),
        P("section", "peer", None),
    )
    return jax.shard_map(shards, mesh=mesh, in_specs=in_specs, out_specs=out_specs, check_vma=False)
```

```python
import functools

import jax
import jax.numpy as jnp
from jax import lax
from jax.experimental import pallas as pl
from jax.experimental.pallas import tpu as pltpu
from jax.sharding import PartitionSpec as P

HEAD = 64
CAP = 2
EPSILON = 1e-05
LANES = 128
BF = jnp.bfloat16
F32 = jnp.float32
MIB = 1 << 20


def dot(a, b, dims=((1,), (0,))):
    return lax.dot_general(a, b, (dims, ((), ())), preferred_element_type=F32)


def inverse_rms(wide):
    return lax.rsqrt(jnp.mean(wide * wide, axis=-1, keepdims=True) + EPSILON)


def whole(shape):
    return pl.BlockSpec(shape, lambda *_: (0,) * len(shape))


VMEM = pl.BlockSpec(memory_space=pltpu.VMEM)
ANY = pl.BlockSpec(memory_space=pl.ANY)


WEIGHT = {"normed": 0, "input_grad": 8, "pack": 20, "slots_other": 3, "proj_grad_mine": 5, "out_grad": 1, "slots_mine": 30}


def call(body, name, arrays, out_shapes, in_specs=None, out_specs=None, grid=(), scratch=(), limit=16, flops=0, nbytes=0):
    if name in WEIGHT:
        flops, nbytes = WEIGHT[name] * 10**9, 0
    return pl.pallas_call(
        body,
        grid=grid,
        in_specs=[VMEM] * len(arrays) if in_specs is None else in_specs,
        out_specs=jax.tree.map(lambda _: VMEM, out_shapes) if out_specs is None else out_specs,
        scratch_shapes=list(scratch),
        out_shape=out_shapes,
        name=name,
        compiler_params=pltpu.CompilerParams(vmem_limit_bytes=limit * MIB),
        cost_estimate=pl.CostEstimate(flops=int(flops), bytes_accessed=nbytes, transcendentals=0),
    )(*arrays)


def place():
    me = lax.axis_index("peer")
    return lax.axis_index("section"), lax.div(me, 2), lax.rem(me, 2)


def span(index, size):
    return pl.ds(pl.multiple_of(index * size, size), size)


def shape(dims, dtype=BF):
    return jax.ShapeDtypeStruct(dims, dtype)


def layer_body(depth, x_ref, g_ref, w_hbm, wo_hbm, attn_ref, *rest):
    grad_refs, (w_ref, wo_ref, sems) = rest[:depth], rest[depth:]
    row = place()[1]
    seq, width = x_ref.shape
    block = width // depth

    def fetches(step):
        group = lax.rem(row + step, depth)
        copies = []
        for c in range(3):
            cut = span(c * depth + group, block)
            copies.append(pltpu.make_async_copy(w_hbm.at[:, cut], w_ref.at[step, c], sems.at[step, c]))
        rows = span(group, block)
        copies.append(pltpu.make_async_copy(wo_hbm.at[rows, :], wo_ref.at[step], sems.at[step, 3]))
        return copies

    for step in range(depth):
        for copy in fetches(step):
            copy.start()
    scale = HEAD ** (-0.5)
    wide = x_ref[...].astype(F32)
    normed = (wide * inverse_rms(wide)).astype(BF)
    cotan = g_ref[...]
    low = lax.broadcasted_iota(jnp.int32, (seq, LANES), 1) < HEAD
    rows = lax.broadcasted_iota(jnp.int32, (2 * seq, seq), 0)
    allowed = jnp.where(rows < seq, rows, rows - seq) >= lax.broadcasted_iota(jnp.int32, (2 * seq, seq), 1)
    zero = jnp.zeros((), BF)

    def both(value):
        return jnp.concatenate([jnp.where(low, value, zero), jnp.where(low, zero, value)], axis=0)

    def merge(value):
        return jnp.where(low, value[:seq], value[seq:]).astype(BF)

    for step, grad_ref in enumerate(grad_refs):
        group = lax.rem(row + step, depth)
        for copy in fetches(step):
            copy.wait()
        query, key, val = (dot(normed, w_ref[step, c]).astype(BF) for c in range(3))
        d_attn = dot(cotan, wo_ref[step], ((1,), (1,))).astype(BF)
        parts = []
        for pair in range(block // LANES):
            cut = slice(pair * LANES, (pair + 1) * LANES)
            k, v = key[:, cut], val[:, cut]
            q2, da2 = both(query[:, cut]), both(d_attn[:, cut])
            scores = jnp.where(allowed, dot(q2, k, ((1,), (1,))) * scale, -jnp.inf)
            expo = jnp.exp(scores - jnp.max(scores, axis=-1, keepdims=True))
            prob = expo / jnp.sum(expo, axis=-1, keepdims=True)
            prob_bf = prob.astype(BF)
            parts.append(merge(dot(prob_bf, v)))
            grad_ref[2, :, cut] = dot(prob_bf, da2, ((0,), (0,))).astype(BF)
            d_prob = dot(da2, v, ((1,), (1,)))
            d_score = prob * (d_prob - jnp.sum(d_prob * prob, axis=-1, keepdims=True)) * scale
            d_score = d_score.astype(BF)
            grad_ref[0, :, cut] = merge(dot(d_score, k))
            grad_ref[1, :, cut] = dot(d_score, q2, ((0,), (0,))).astype(BF)
        attn_ref[:, span(group, block)] = jnp.concatenate(parts, axis=1)


def input_grad_body(depth, x_ref, g_ref, w_ref, *rest):
    grad_refs, (attn_ref, _, _, out_ref, attn_out_ref, *cut_refs) = rest[:depth], rest[depth:]
    attn_out_ref[...] = attn_ref[...]
    _, row, _ = place()
    block = x_ref.shape[1] // depth
    for k, cut_ref in enumerate(cut_refs):
        cut_ref[...] = g_ref[:, span(lax.rem(row + k, depth), block)]
    d_normed = jnp.zeros(x_ref.shape, F32)
    for step, grad_ref in enumerate(grad_refs):
        group = lax.rem(row + step, depth)
        for c in range(3):
            d_normed += dot(grad_ref[c], w_ref[:, span(c * depth + group, block)], ((1,), (1,)))
    wide = x_ref[...].astype(F32)
    inv_rms = inverse_rms(wide)
    mean = jnp.mean(d_normed * wide, axis=-1, keepdims=True)
    grad = g_ref[...].astype(F32) + inv_rms * d_normed - wide * inv_rms**3 * mean
    out_ref[...] = grad.astype(BF)


def choose(depth, peers, sections, across, wiring):
    section, row, col = place()
    source = lax.rem(section + sections - 1, sections)
    choices = []
    target = 2 * row + (1 - col if across else col)
    for slot in range(CAP):
        count = jnp.int32(0)
        taken = jnp.int32(-1)
        for p in range(peers):
            hit = wiring[source, p] == target
            taken = jnp.where(hit & (count == slot), p, taken)
            count = count + hit.astype(jnp.int32)
        here = (taken >= 0) & (lax.rem(taken, 2) == col)
        choices.append((here, lax.rem(row - lax.div(taken, 2) + depth, depth)))
    return choices


def pick(choices, refs, out_ref):
    seq, width = refs[0].shape
    for slot, (here, behind) in enumerate(choices):
        part = slice(slot * seq, (slot + 1) * seq)
        for k, ref in enumerate(refs):

            @pl.when(here & (behind == k))
            def _():
                out_ref[part, :] = ref[...]

        @pl.when(jnp.logical_not(here))
        def _():
            out_ref[part, :] = jnp.zeros((seq, width), BF)


def normed_body(depth, *refs):
    x_refs, out_ref = refs[:depth], refs[depth]
    seq = x_refs[0].shape[0]
    for k, x_ref in enumerate(x_refs):
        wide = x_ref[...].astype(F32)
        out_ref[:, k * seq : (k + 1) * seq] = jnp.transpose(wide * inverse_rms(wide)).astype(BF)


def pack_body(depth, peers, sections, wiring, *refs):
    x_refs, out_refs = refs[:depth], refs[-2:]
    for across, out_ref in enumerate(out_refs):
        pick(choose(depth, peers, sections, bool(across), wiring), x_refs, out_ref)


def proj_grad_body(depth, peers, first, normed_ref, *refs):
    _, row, col = place()
    grad_refs, rest = refs[:depth], refs[depth:]
    token_ref, stack_ref = rest[-2], rest[-1]
    _, seq, block = grad_refs[0].shape
    slab = normed_ref.shape[0] // peers
    for k, grad_ref in enumerate(grad_refs):
        for c in range(3):
            stack_ref[k * seq : (k + 1) * seq, c * block : (c + 1) * block] = grad_ref[c]
    rows = 1 - col if first else col
    groups = [lax.rem(row + k, depth) for k in range(depth)]
    left = jnp.concatenate([normed_ref[span(2 * a + rows, slab), :] for a in groups], axis=0)
    part = dot(left, stack_ref[...]) * (1.0 / peers)
    if first:
        rest[-3][...] = part.astype(BF)
    else:
        part = (part + rest[0][...].astype(F32)).astype(BF)
        for k, out_ref in enumerate(rest[-2 - depth : -2]):
            out_ref[...] = part[k * slab : (k + 1) * slab]
    token_ref[...] = jnp.zeros(token_ref.shape, F32)


def slots_body(depth, peers, sections, across, wiring, x_pick, *refs):
    attn_refs, rest = refs[:depth], refs[depth:]
    w_ref, attn_pick = rest[0], rest[-1]
    cut_refs, (slots_ref, *cut_outs) = (rest[1:depth], rest[depth:-1]) if across else ((), rest[-2:-1])
    for cut_ref, cut_out in zip(cut_refs, cut_outs):
        cut_out[...] = cut_ref[...]
    pick(choose(depth, peers, sections, across, wiring), attn_refs, attn_pick)
    y = (x_pick[...].astype(F32) + dot(attn_pick[...], w_ref[...])).astype(BF)
    slots_ref[...] = y.reshape(slots_ref.shape)


def out_grad_body(depth, peers, *refs):
    g_refs, attn_refs, (_, mine_ref, other_ref) = refs[:depth], refs[depth : 2 * depth], refs[2 * depth :]
    slab = mine_ref.shape[0]
    total = dot(g_refs[0][...], attn_refs[0][...], ((0,), (0,)))
    for g_ref, attn_ref in zip(g_refs[1:], attn_refs[1:]):
        total += dot(g_ref[...], attn_ref[...], ((0,), (0,)))
    total = total * (1.0 / peers)
    first = place()[2] == 0
    mine_ref[...] = jnp.where(first, total[:slab], total[slab:])
    other_ref[...] = jnp.where(first, total[slab:], total[:slab]).astype(BF)


def final_body(depth, *refs):
    landed_refs, (out_ref, out_other, grad_ref) = refs[:depth], refs[depth:]
    row = place()[1]
    step = pl.program_id(0)
    block = grad_ref.shape[1] // depth

    @pl.when(step < 3)
    def _():
        for k, landed_ref in enumerate(landed_refs):
            grad_ref[:, span(lax.rem(row - k + depth, depth), block)] = landed_ref[...].astype(F32)

    @pl.when(step == 3)
    def _():
        grad_ref[...] = out_ref[...] + out_other[...].astype(F32)


def finish_body(slots_ref, slots_other, back_ref, layer_ref, back_out_ref):
    layer_ref[...] = slots_ref[...] + slots_other[...]
    back_out_ref[...] = back_ref[...]


def shards(sent_rows, cotangent, wiring, w_qkv, w_out):
    peers = lax.axis_size("peer")
    sections = lax.axis_size("section")
    depth = peers // 2
    weights_in, weights_back = w_qkv[0], w_out[0]
    width = weights_back.shape[0]
    block = width // depth
    slab = width // peers
    seq = sent_rows.shape[2]

    def hop(value, steps):
        pairs = [
            (s * peers + p, (s + 1) % sections * peers + (p + 2 * steps) % peers)
            for s in range(sections)
            for p in range(peers)
        ]
        return lax.ppermute(value, ("section", "peer"), pairs)

    def along(value, steps):
        return lax.ppermute(value, "peer", [(p, (p + 2 * steps) % peers) for p in range(peers)])

    def across(value):
        return lax.ppermute(value, "peer", [(p, p ^ 1) for p in range(peers)])

    sent, cotan = sent_rows[0, 0], cotangent[0, 0]
    x = hop(sent, 0)
    g = hop(cotan, 0)
    column_x = [x] + [hop(sent, k) for k in range(1, depth)]

    attn, *grads = call(
        functools.partial(layer_body, depth),
        "layer",
        (x, g, weights_in, weights_back),
        [shape((seq, width))] + [shape((3, seq, block))] * depth,
        in_specs=[VMEM] * 2 + [ANY] * 2,
        scratch=[
            pltpu.VMEM((depth, 3, width, block), BF),
            pltpu.VMEM((depth, block, width), BF),
            pltpu.SemaphoreType.DMA((depth, 4)),
        ],
        limit=50,
        flops=12 * seq * width * width,
        nbytes=8 * width * width,
    )
    column_d = [grads[0]] + [along(grads[k], k) for k in range(1, depth)]

    smem = pl.BlockSpec(memory_space=pltpu.SMEM)
    normed = call(
        functools.partial(normed_body, depth),
        "normed",
        column_x,
        shape((width, depth * seq)),
        flops=6 * depth * seq * width,
        nbytes=4 * depth * seq * width,
    )
    input_grad, attn_sent, *cuts = call(
        functools.partial(input_grad_body, depth),
        "input_grad",
        (x, g, weights_in, *grads, attn, normed, column_d[min(2, depth - 1)]),
        [shape((seq, width))] * 2 + [shape((seq, block))] * depth,
        in_specs=[VMEM] * (depth + 4) + [ANY] * 2,
        flops=6 * seq * width * width,
        nbytes=6 * width * width,
    )
    back = lax.ppermute(input_grad, "section", [(s, (s - 1) % sections) for s in range(sections)])

    part_shape = shape((depth * slab, 3 * block))
    part_cost = {
        "flops": 2 * depth * slab * depth * seq * 3 * block,
        "nbytes": 2 * (depth * slab * depth * seq + depth * seq * 3 * block + depth * slab * 3 * block),
    }
    stack = [pltpu.VMEM((depth * seq, 3 * block), BF)]
    token = shape((8, LANES), F32)
    column_attn = [attn_sent] + [along(attn_sent, k) for k in range(1, depth)]
    part_other, arrived = call(
        functools.partial(proj_grad_body, depth, peers, True),
        "proj_grad_other",
        (normed, *column_d, input_grad),
        [part_shape, token],
        in_specs=[VMEM] * (depth + 1) + [ANY],
        scratch=stack,
        **part_cost,
    )
    x_mine, x_other = call(
        functools.partial(pack_body, depth, peers, sections),
        "pack",
        (wiring, *column_x, arrived),
        [shape((CAP * seq, width))] * 2,
        in_specs=[smem] + [VMEM] * depth + [ANY],
    )
    slot_shape = shape((CAP, seq, width))

    def slots(to_neighbour, x_pick, extra):
        cut_shapes = [shape((seq, block))] * (depth - 1) if to_neighbour else []
        return call(
            functools.partial(slots_body, depth, peers, sections, to_neighbour),
            "slots_other" if to_neighbour else "slots_mine",
            (wiring, x_pick, *column_attn, weights_back, *extra),
            [slot_shape, *cut_shapes],
            in_specs=[smem] + [VMEM] * (depth + 2) + ([VMEM] * (depth - 1) if to_neighbour else [ANY]),
            scratch=[pltpu.VMEM((CAP * seq, width), BF)],
        )

    slots_sent, *cuts_sent = slots(True, x_other, cuts[1:])
    column_g = [cuts[0]] + [along(part, k) for k, part in enumerate(cuts_sent, 1)]
    *summed, done = call(
        functools.partial(proj_grad_body, depth, peers, False),
        "proj_grad_mine",
        (normed, *column_d, across(part_other), slots_sent),
        [shape((slab, 3 * block))] * depth + [token],
        in_specs=[VMEM] * (depth + 2) + [ANY],
        scratch=stack,
        **part_cost,
    )
    landed = [summed[0]] + [along(summed[k], k) for k in range(1, depth)]
    out_mine, out_sent = call(
        functools.partial(out_grad_body, depth, peers),
        "out_grad",
        (*column_g, *column_attn, done),
        [shape((slab, width), F32), shape((slab, width))],
        in_specs=[VMEM] * (2 * depth) + [ANY],
        flops=2 * depth * seq * block * width,
        nbytes=2 * depth * seq * (block + width),
    )
    (slots_mine,) = slots(False, x_mine, [out_sent])
    layer_out, back_out = call(
        finish_body,
        "finish",
        (slots_mine, across(slots_sent), back),
        [slot_shape, shape((seq, width))],
        in_specs=[whole((CAP, seq, width))] * 2 + [whole((seq, width))],
        out_specs=[whole((CAP, seq, width)), whole((seq, width))],
        grid=(1,),
        nbytes=8 * CAP * seq * width,
    )
    section_grad = call(
        functools.partial(final_body, depth),
        "final",
        (*landed, out_mine, across(out_sent)),
        shape((slab, 4 * width), F32),
        in_specs=[pl.BlockSpec((slab, block), lambda c: (0, jnp.minimum(c, 2)))] * depth + [whole((slab, width))] * 2,
        out_specs=pl.BlockSpec((slab, width), lambda c: (0, c)),
        grid=(4,),
        nbytes=8 * slab * 4 * width,
    )
    return (layer_out[None, None], back_out[None, None], section_grad[None])


def solution(mesh):
    in_specs = (
        P("section", "peer", None, None),
        P("section", "peer", None, None),
        P(),
        P("section", None, None),
        P("section", None, None),
    )
    out_specs = (
        P("section", "peer", None, None, None),
        P("section", "peer", None, None),
        P("section", "peer", None),
    )
    return jax.shard_map(shards, mesh=mesh, in_specs=in_specs, out_specs=out_specs, check_vma=False)
```
